128 devices in a mesh: section: 2 (over x_lo), mp: 16 (over z, y), dp: 4 (over x_hi, core).
Axes of the slice: x: 4 (x_hi: 2, x_lo: 2; x = x_hi * 2 + x_lo), y: 4, z: 4, core: 2. Of those that a mesh axis runs over, the one named last changes fastest.
Arguments:
- layer_input: bfloat16 [2, 1024, 2048], P(None, 'dp', 'mp'), may hold values from -6 to 6
- out_cotangent: float32 [2, 1024, 2048], P(None, 'dp', 'mp'), may hold values from -6 to 6
- doc_lengths: int32 [2, 4], replicated, may hold values from 1 to 1021, as said below
- query_weight: bfloat16 [2048, 2048], P('dp', 'mp'), may hold values from -0.125 to 0.125
- key_weight: bfloat16 [2048, 2048], P('dp', 'mp'), may hold values from -0.125 to 0.125
- value_weight: bfloat16 [2048, 2048], P('dp', 'mp'), may hold values from -0.125 to 0.125
- query_bias: float32 [2048], P('mp'), may hold values from -1.5 to 1.5
- value_bias: float32 [2048], P('mp'), may hold values from -1.5 to 1.5
- output_weight: bfloat16 [2048, 2048], P('mp', 'dp'), may hold values from -3 to 3
- output_bias: float32 [2048], P('mp'), may hold values from -1.5 to 1.5
- attention_norm_gain: float32 [2048], P('mp'), may hold values from 0.25 to 1.75
- attention_norm_shift: float32 [2048], P('mp'), may hold values from -1.5 to 1.5
- hidden_weight: bfloat16 [2048, 8192], P('dp', 'mp'), may hold values from -0.125 to 0.125
- hidden_bias: float32 [8192], P('mp'), may hold values from -1.5 to 1.5
- proj_weight: bfloat16 [8192, 2048], P('mp', 'dp'), may hold values from -0.0625 to 0.0625
- proj_bias: float32 [2048], P('mp'), may hold values from -1.5 to 1.5
- closing_norm_gain: float32 [2048], P('mp'), may hold values from 0.25 to 1.75
- closing_norm_shift: float32 [2048], P('mp'), may hold values from -1.5 to 1.5
Outputs:
- boundary: float32 [2, 2, 1024, 2048], P('section', None, 'dp', 'mp')
- query_weight_grad: float32 [2048, 2048], P('dp', 'mp')
- key_weight_grad: float32 [2048, 2048], P('dp', 'mp')
- value_weight_grad: float32 [2048, 2048], P('dp', 'mp')
- query_bias_grad: float32 [2048], P('mp')
- value_bias_grad: float32 [2048], P('mp')
- output_weight_grad: float32 [2048, 2048], P('mp', 'dp')
- output_bias_grad: float32 [2048], P('mp')
- attn_gain_grad: float32 [2048], P('mp')
- attn_shift_grad: float32 [2048], P('mp')
- hidden_weight_grad: float32 [2048, 8192], P('dp', 'mp')
- hidden_bias_grad: float32 [8192], P('mp')
- proj_weight_grad: float32 [8192, 2048], P('mp', 'dp')
- proj_bias_grad: float32 [2048], P('mp')
- final_gain_grad: float32 [2048], P('mp')
- final_shift_grad: float32 [2048], P('mp')
The draws below stay inside these ranges and needn't reach their ends.
Inputs may be any that keep to these rules, and one draw needn't show every extreme that they name: `doc_lengths`: each row holds the lengths of 4 documents packed in order into one sequence; they sum to 1024; the second document begins within the first 256 tokens and ends within the last 256 tokens.
All inputs are finite; a program needn't handle non-finite values.
Results may differ from the reference program's by a relative error of at most 0.03.
Values may be sent and summed in bfloat16 or wider, within the bound.
No kernel may reach another device: no remote copies, remote signals or barrier semaphores. Data moves between devices by JAX's collectives and lax.ppermute only.
A program may use at most 128 MiB of HBM per device.

```python
import math
import jax
import jax.numpy as jnp
from jax import lax

MODEL_WIDTH = 2048
HEADS = 16
HEAD = 128
FF = 8192
TOK_DEV = 256
MICRO = 2
SEQ = 1024


def draw_doc_lengths(key, part):
    key = jax.random.fold_in(key, 7)
    key_one, key_two, key_three, key_four = jax.random.split(key, 4)
    first_len = jax.random.randint(key_one, (MICRO,), 1, TOK_DEV)
    third_len = jax.random.randint(key_two, (MICRO,), 1, TOK_DEV // 2)
    fourth_len = jax.random.randint(key_three, (MICRO,), 1, TOK_DEV // 2)
    chosen = jax.random.randint(key_four, (), 0, MICRO)
    picked = jnp.arange(MICRO) == chosen
    first_len = jnp.where(picked, 1, first_len)
    third_len = jnp.where(picked, 1, third_len)
    fourth_len = jnp.where(picked, 1, fourth_len)
    second_len = SEQ - first_len - third_len - fourth_len
    return jnp.stack([first_len, second_len, third_len, fourth_len], axis=1).astype(jnp.int32)


def block_levels(rng, dims, cuts, smallest, largest):
    gain, own = 1.0, jax.random.fold_in(rng, 6)
    for dim, parts in cuts:
        draws = jnp.exp(jax.random.uniform(jax.random.fold_in(own, dim), (parts,), jnp.float32, smallest / len(cuts), largest / len(cuts)))
        gain = gain * jnp.repeat(draws, dims[dim] // parts).reshape([-1 if axis == dim else 1 for axis in range(len(dims))])
    return gain


def scatter_about(stream_key, extent, scale, limit, pieces=(), kind=jnp.bfloat16):
    drawn = scale * jax.random.normal(stream_key, extent, jnp.float32)
    if pieces:
        drawn = drawn * block_levels(stream_key, extent, pieces, -0.22, 0.18)
    return jnp.clip(drawn, -limit, limit).astype(kind)


def setup_inputs(seed: int = 0) -> dict:
    key_of = jax.random.split(jax.random.key(seed), 19)
    return {
        "layer_input": scatter_about(key_of[0], (MICRO, SEQ, MODEL_WIDTH), 1.0, 6.0, ((1, 4), (2, 16))),
        "out_cotangent": scatter_about(key_of[1], (MICRO, SEQ, MODEL_WIDTH), 1.0, 6.0, ((1, 4), (2, 16)), jnp.float32),
        "doc_lengths": draw_doc_lengths(jax.random.fold_in(key_of[18], 71), 0),
        "query_weight": scatter_about(key_of[3], (MODEL_WIDTH, MODEL_WIDTH), MODEL_WIDTH ** -0.5, 0.125, ((0, 4), (1, 16))),
        "key_weight": scatter_about(key_of[4], (MODEL_WIDTH, MODEL_WIDTH), MODEL_WIDTH ** -0.5, 0.125, ((0, 4), (1, 16))),
        "value_weight": scatter_about(key_of[5], (MODEL_WIDTH, MODEL_WIDTH), MODEL_WIDTH ** -0.5, 0.125, ((0, 4), (1, 16))),
        "query_bias": scatter_about(key_of[6], (MODEL_WIDTH,), 0.3, 1.5, ((0, 16),), jnp.float32),
        "value_bias": scatter_about(key_of[7], (MODEL_WIDTH,), 0.3, 1.5, ((0, 16),), jnp.float32),
        "output_weight": scatter_about(key_of[8], (MODEL_WIDTH, MODEL_WIDTH), (max(2 * MODEL_WIDTH // SEQ, 1)) ** -0.5, 3.0, ((0, 16), (1, 4))),
        "output_bias": scatter_about(key_of[9], (MODEL_WIDTH,), 0.3, 1.5, ((0, 16),), jnp.float32),
        "attention_norm_gain": jnp.clip(1.0 + 0.15 * jax.random.normal(key_of[10], (MODEL_WIDTH,), jnp.float32), 0.25, 1.75),
        "attention_norm_shift": scatter_about(key_of[11], (MODEL_WIDTH,), 0.3, 1.5, ((0, 16),), jnp.float32),
        "hidden_weight": scatter_about(key_of[12], (MODEL_WIDTH, FF), MODEL_WIDTH ** -0.5, 0.125, ((0, 4), (1, 16))),
        "hidden_bias": scatter_about(key_of[13], (FF,), 0.3, 1.5, ((0, 16),), jnp.float32),
        "proj_weight": scatter_about(key_of[14], (FF, MODEL_WIDTH), FF ** -0.5, 0.0625, ((0, 16), (1, 4))),
        "proj_bias": scatter_about(key_of[15], (MODEL_WIDTH,), 0.3, 1.5, ((0, 16),), jnp.float32),
        "closing_norm_gain": jnp.clip(1.0 + 0.15 * jax.random.normal(key_of[16], (MODEL_WIDTH,), jnp.float32), 0.25, 1.75),
        "closing_norm_shift": scatter_about(key_of[17], (MODEL_WIDTH,), 0.3, 1.5, ((0, 16),), jnp.float32),
    }


@jax.custom_vjp
def low(v):
    return lax.optimization_barrier(v.astype(jnp.bfloat16)).astype(jnp.float32)

@jax.custom_vjp
def low_back(v):
    return v

def low_keep(v):
    return (low(v), None)

def low_pass(kept, grad):
    return (grad,)

def back_keep(v):
    return (v, None)

def back_low(kept, grad):
    return (low(grad),)
low.defvjp(low_keep, low_pass)
low_back.defvjp(back_keep, back_low)

def matmul_high(left, right):
    return jnp.dot(left, right, precision=lax.Precision.HIGHEST, preferred_element_type=jnp.float32)

def both_round(value):
    return low(low_back(value))

def normalize(residual_first, norm_gain, norm_shift):
    center = residual_first - lax.optimization_barrier(jnp.mean(residual_first, axis=-1, keepdims=True))
    spread = lax.optimization_barrier(jnp.mean(center * center, axis=-1, keepdims=True))
    return center * lax.rsqrt(spread + 1e-06) * norm_gain + norm_shift

def segment_ids(row):
    bounds = jnp.cumsum(row).astype(jnp.int32)
    places = jnp.arange(SEQ, dtype=jnp.int32)
    return lax.optimization_barrier(jnp.sum((places[:, None] >= bounds[None, :]).astype(jnp.int32), axis=1))

def same_of(row):
    labels = segment_ids(row)
    return labels[:, None] == labels[None, :]

def layer(hidden, same, params):
    query_weight, key_weight, value_weight, query_bias, value_bias, output_weight, output_bias, attention_norm_gain, attention_norm_shift, hidden_weight, hidden_bias, proj_weight, proj_bias, closing_norm_gain, closing_norm_shift = params
    acts = low(hidden)
    query = both_round(matmul_high(acts, query_weight) + query_bias).reshape(SEQ, HEADS, HEAD)
    keys = both_round(matmul_high(acts, key_weight)).reshape(SEQ, HEADS, HEAD)
    values = both_round(matmul_high(acts, value_weight) + value_bias).reshape(SEQ, HEADS, HEAD)
    scores = jnp.einsum('qhd,khd->hqk', query, keys, precision=lax.Precision.HIGHEST) * (1.0 / math.sqrt(HEAD))
    scores = low_back(scores)
    scores = jnp.where(same[None], scores, -1e+30)
    top = lax.optimization_barrier(jnp.max(scores, axis=-1, keepdims=True))
    expo = jnp.exp(scores - top)
    probs = low(expo / lax.optimization_barrier(jnp.sum(expo, axis=-1, keepdims=True)))
    mixed = jnp.einsum('hqk,khd->qhd', probs, values, precision=lax.Precision.HIGHEST).reshape(SEQ, MODEL_WIDTH)
    mixed = both_round(mixed)
    residual_first = hidden + low_back(matmul_high(mixed, output_weight)) + output_bias
    normed_rows = normalize(residual_first, attention_norm_gain, attention_norm_shift)
    inner = low_back(matmul_high(low(normed_rows), hidden_weight) + hidden_bias)
    active = low(jax.nn.gelu(inner, approximate=True))
    residual_second = normed_rows + low_back(matmul_high(active, proj_weight)) + proj_bias
    return normalize(residual_second, closing_norm_gain, closing_norm_shift)

def reference(layer_input, out_cotangent, doc_lengths, query_weight, key_weight, value_weight, query_bias, value_bias, output_weight, output_bias, attention_norm_gain, attention_norm_shift, hidden_weight, hidden_bias, proj_weight, proj_bias, closing_norm_gain, closing_norm_shift):
    sames = lax.map(same_of, doc_lengths)
    params = tuple((item.astype(jnp.float32) for item in (query_weight, key_weight, value_weight, query_bias, value_bias, output_weight, output_bias, attention_norm_gain, attention_norm_shift, hidden_weight, hidden_bias, proj_weight, proj_bias, closing_norm_gain, closing_norm_shift)))

    def forward(start, *weights):

        def one_batch(pair):
            return layer(layer(pair[0], pair[1], weights), pair[1], weights)
        return lax.map(jax.checkpoint(one_batch), (start, sames))
    ends, pull = jax.vjp(forward, layer_input.astype(jnp.float32), *params)
    grads = pull(out_cotangent.astype(jnp.float32))
    boundary = jnp.stack([grads[0], ends])
    return (boundary, grads[1], grads[2], grads[3], grads[4], grads[5], grads[6], grads[7], grads[8], grads[9], grads[10], grads[11], grads[12], grads[13], grads[14], grads[15])
```

```python
import math

import jax
import jax.numpy as jnp
from jax import lax
from jax.sharding import PartitionSpec as P

WIDTH = 2048
HEAD = 128
SCALE = 1.0 / math.sqrt(HEAD)
EPS = 1e-06
BF = jnp.bfloat16
F32 = jnp.float32


def core_swap(array):
    count = lax.axis_size("dp")
    return lax.ppermute(array, "dp", [(i, i ^ 1) for i in range(count)])


def chip_swap(array):
    count = lax.axis_size("dp")
    route = [(s * count + i, (1 - s) * count + (i ^ 2)) for s in range(2) for i in range(count)]
    return lax.ppermute(array, ("section", "dp"), route)


def section_swap(array):
    return lax.ppermute(array, "section", [(0, 1), (1, 0)])


def exchange(pieces):
    return lax.all_to_all(pieces, "mp", split_axis=0, concat_axis=0, tiled=True)


def rows_to_all(rows):
    parts = lax.axis_size("mp")
    copies = jnp.broadcast_to(rows, (parts, *rows.shape))
    return exchange(copies).reshape(parts * rows.shape[0], rows.shape[1])


def row_sums(partial):
    parts = lax.axis_size("mp")
    pieces = partial.astype(BF).reshape(parts, -1, partial.shape[1])
    return jnp.sum(exchange(pieces).astype(F32), axis=0)


def four_blocks(own):
    far = chip_swap(own)
    return own, core_swap(own), far, core_swap(far)


def laid_in_order(blocks, axis, part):
    length = blocks[0].shape[axis]
    shape = list(blocks[0].shape)
    shape[axis] = length * len(blocks)
    whole = jnp.zeros(shape, blocks[0].dtype)
    for k, block in enumerate(blocks):
        whole = lax.dynamic_update_slice_in_dim(whole, block, (part ^ k) * length, axis)
    return whole


def block_of(whole, axis, index):
    length = whole.shape[axis] // 4
    return lax.dynamic_slice_in_dim(whole, index * length, length, axis)


def owner_sums(cut):
    near = cut(0) + core_swap(cut(1).astype(BF)).astype(F32)
    far = cut(2) + core_swap(cut(3).astype(BF)).astype(F32)
    both = near + chip_swap(far.astype(BF)).astype(F32)
    low = both.astype(BF)
    return both + section_swap(low).astype(F32)


def small_sums(vector):
    vector = vector + core_swap(vector)
    vector = vector + chip_swap(vector)
    return vector + section_swap(vector)


def in_terms(value):
    high = lax.reduce_precision(value, 8, 7)
    rest = value - high
    middle = lax.reduce_precision(rest, 8, 7)
    low = rest - middle
    return jnp.concatenate([high.astype(BF), middle.astype(BF), low.astype(BF)], axis=-2)


def from_terms(terms):
    rows = terms.shape[-2] // 3
    high, middle, low = (terms[..., k * rows : (k + 1) * rows, :].astype(F32) for k in range(3))
    return high + (middle + low)


def norm(rows, gain, shift):
    mean = jnp.mean(rows, axis=-1, keepdims=True)
    centered = rows - mean
    rstd = lax.rsqrt(jnp.mean(centered * centered, axis=-1, keepdims=True) + EPS)
    standard = centered * rstd
    return standard * gain + shift, standard, rstd


def norm_back(grad, standard, rstd, gain):
    scaled = grad * gain
    mean = jnp.mean(scaled, axis=-1, keepdims=True)
    cross = jnp.mean(scaled * standard, axis=-1, keepdims=True)
    back = rstd * (scaled - mean - standard * cross)
    return back, jnp.sum(grad * standard, axis=0), jnp.sum(grad, axis=0)


def dot(left, right):
    return jnp.dot(left, right, preferred_element_type=F32)


def dot_t(left, right):
    return lax.dot_general(left, right, (((1,), (1,)), ((), ())), preferred_element_type=F32)


def t_dot(left, right):
    return lax.dot_general(left, right, (((0,), (0,)), ((), ())), preferred_element_type=F32)


def gelu(value):
    return jax.nn.gelu(value, approximate=True)


def probabilities(query, keys, same):
    scores = jnp.where(same, dot_t(query, keys) * SCALE, -1e30)
    expo = jnp.exp(scores - jnp.max(scores, axis=-1, keepdims=True))
    return expo / jnp.sum(expo, axis=-1, keepdims=True)


def forward_layer(rows, acts, same, weights):
    qkv_weight, out_weight, in_weight, down_weight = weights["qkv"], weights["out"], weights["in"], weights["down"]
    projected = dot(acts, qkv_weight)
    query = (projected[:, :HEAD] + weights["query_bias"]).astype(BF)
    keys = projected[:, HEAD : 2 * HEAD].astype(BF)
    values = (projected[:, 2 * HEAD :] + weights["value_bias"]).astype(BF)
    pairs = jnp.concatenate(four_blocks(jnp.concatenate([keys, values], axis=1)), axis=0)
    probs = probabilities(query, pairs[:, :HEAD], same)
    mixed = dot(probs.astype(BF), pairs[:, HEAD:]).astype(BF)
    first = rows + row_sums(dot(mixed, out_weight)) + weights["output_bias"]
    normed, standard_one, rstd_one = norm(first, weights["attn_gain"], weights["attn_shift"])
    normed_full = rows_to_all(normed.astype(BF))
    inner = dot(normed_full, in_weight) + weights["hidden_bias"]
    active = gelu(inner).astype(BF)
    second = normed + row_sums(dot(active, down_weight)) + weights["proj_bias"]
    result, standard_two, rstd_two = norm(second, weights["closing_gain"], weights["closing_shift"])
    saved = (acts, query, pairs, probs, mixed, standard_one, rstd_one, normed_full, inner, active, standard_two, rstd_two)
    return result, saved


def backward_layer(grad, saved, weights):
    acts, query, pairs, probs, mixed, standard_one, rstd_one, normed_full, inner, active, standard_two, rstd_two = saved
    grad_two, closing_gain, closing_shift = norm_back(grad, standard_two, rstd_two, weights["closing_gain"])
    grad_two_full = rows_to_all(grad_two.astype(BF))
    pull = jax.vjp(gelu, inner)[1]
    inner_grad = pull(dot_t(grad_two_full, weights["down"]))[0].astype(BF)
    normed_grad = grad_two + row_sums(dot_t(inner_grad, weights["in"]))
    grad_one, attn_gain, attn_shift = norm_back(normed_grad, standard_one, rstd_one, weights["attn_gain"])
    grad_one_full = rows_to_all(grad_one.astype(BF))
    mixed_grad = dot_t(grad_one_full, weights["out"]).astype(BF)
    keys, values = pairs[:, :HEAD], pairs[:, HEAD:]
    value_terms = t_dot(probs.astype(BF), mixed_grad)
    prob_grad = dot_t(mixed_grad, values)
    score_grad = (probs * (prob_grad - jnp.sum(probs * prob_grad, axis=-1, keepdims=True))).astype(BF)
    query_grad = (dot(score_grad, keys) * SCALE).astype(BF)
    key_terms = t_dot(score_grad, query) * SCALE
    terms = jnp.concatenate([key_terms, value_terms], axis=1)
    half = terms.shape[0] // 2
    near = terms[:half] + chip_swap(terms[half:].astype(BF)).astype(F32)
    rows = half // 2
    pair_grad = (near[:rows] + core_swap(near[rows:])).astype(BF)
    qkv_grad = jnp.concatenate([query_grad, pair_grad], axis=1)
    vectors = jnp.stack(
        [jnp.sum(grad_one, axis=0), attn_gain, attn_shift, jnp.sum(grad_two, axis=0), closing_gain, closing_shift]
    )
    local = jnp.concatenate(
        [
            jnp.sum(inner_grad.astype(F32), axis=0),
            jnp.sum(query_grad.astype(F32), axis=0),
            jnp.sum(pair_grad[:, HEAD:].astype(F32), axis=0),
        ]
    )
    large = ((acts, qkv_grad), (mixed, grad_one_full), (normed_full, inner_grad), (active, grad_two_full))
    return grad_one, dot_t(qkv_grad, weights["qkv"]), vectors, local, large


def body(
    layer_input,
    out_cotangent,
    doc_lengths,
    query_weight,
    key_weight,
    value_weight,
    query_bias,
    value_bias,
    output_weight,
    output_bias,
    attention_norm_gain,
    attention_norm_shift,
    hidden_weight,
    hidden_bias,
    proj_weight,
    proj_bias,
    closing_norm_gain,
    closing_norm_shift,
):
    section = lax.axis_index("section")
    part = lax.axis_index("dp")
    place = lax.axis_index("mp")
    parts = lax.axis_size("mp")
    batch = section ^ (part // 2)
    tokens, features = layer_input.shape[1:]
    own_rows = tokens // parts

    qkv_blocks = four_blocks(jnp.concatenate([query_weight, key_weight, value_weight], axis=1))
    rest_blocks = four_blocks(jnp.concatenate([output_weight, hidden_weight, proj_weight], axis=0))
    heads_here = output_weight.shape[0]
    hidden_end = heads_here + hidden_weight.shape[0]

    own_input = lax.dynamic_index_in_dim(layer_input, batch, 0, keepdims=False)
    own_cotangent = lax.dynamic_index_in_dim(out_cotangent, batch, 0, keepdims=False)
    vectors = jnp.stack(
        [output_bias, attention_norm_gain, attention_norm_shift, proj_bias, closing_norm_gain, closing_norm_shift]
    )
    count = vectors.shape[0]
    pieces = jnp.concatenate(
        [
            jnp.broadcast_to(own_input, (parts, tokens, features)),
            in_terms(own_cotangent.reshape(parts, own_rows, features)),
            jnp.broadcast_to(in_terms(vectors), (parts, 3 * count, features)),
        ],
        axis=1,
    )
    pieces = jnp.pad(pieces, ((0, 0), (0, -pieces.shape[1] % 16), (0, 0)))
    arrived = exchange(pieces)

    def side_by_side(stack):
        return jnp.moveaxis(stack, 0, 1).reshape(stack.shape[1], parts * features)

    acts = side_by_side(arrived[:, :tokens])
    cotangent = side_by_side(from_terms(arrived[:, tokens : tokens + 3 * own_rows]))
    vectors = side_by_side(from_terms(arrived[:, tokens + 3 * own_rows : tokens + 3 * own_rows + 3 * count]))
    rows = lax.dynamic_slice_in_dim(acts, place * own_rows, own_rows, 0).astype(F32)

    weights = {
        "qkv": laid_in_order(qkv_blocks, 0, part),
        "out": laid_in_order([block[:heads_here] for block in rest_blocks], 1, part),
        "in": laid_in_order([block[heads_here:hidden_end] for block in rest_blocks], 0, part),
        "down": laid_in_order([block[hidden_end:] for block in rest_blocks], 1, part),
        "query_bias": query_bias,
        "value_bias": value_bias,
        "hidden_bias": hidden_bias,
        "output_bias": vectors[0],
        "attn_gain": vectors[1],
        "attn_shift": vectors[2],
        "proj_bias": vectors[3],
        "closing_gain": vectors[4],
        "closing_shift": vectors[5],
    }

    bounds = jnp.cumsum(lax.dynamic_index_in_dim(doc_lengths, batch, 0, keepdims=False))

    def labels(block):
        places = block * tokens + jnp.arange(tokens, dtype=jnp.int32)
        return jnp.sum((places[:, None] >= bounds[None, :]).astype(jnp.int32), axis=1)

    key_labels = jnp.concatenate([labels(part ^ k) for k in range(4)])
    same = labels(part)[:, None] == key_labels[None, :]

    first_rows, first_saved = forward_layer(rows, acts, same, weights)
    last_rows, last_saved = forward_layer(first_rows, rows_to_all(first_rows.astype(BF)), same, weights)

    grad_one, partial, last_vectors, last_local, last_large = backward_layer(cotangent, last_saved, weights)
    middle_grad = grad_one + row_sums(partial)
    grad_one, partial, first_vectors, first_local, first_large = backward_layer(middle_grad, first_saved, weights)

    def weight_grad(index):
        return t_dot(*last_large[index]) + t_dot(*first_large[index])

    grads = [weight_grad(index) for index in range(4)]
    down_grad = owner_sums(lambda k: block_of(grads[3], 1, part ^ k))
    in_grad = owner_sums(lambda k: block_of(grads[2], 0, part ^ k))
    out_grad = owner_sums(lambda k: block_of(grads[1], 1, part ^ k))
    qkv_grad = owner_sums(lambda k: block_of(grads[0], 0, part ^ k))
    vector_sums = small_sums(last_vectors + first_vectors)
    local_sums = small_sums(last_local + first_local)

    def by_features(array):
        return jnp.moveaxis(array.reshape(array.shape[0], parts, features), 1, 0)

    pieces = jnp.concatenate(
        [
            by_features(partial.astype(BF)),
            in_terms(by_features(grad_one)),
            in_terms(by_features(last_rows)),
            in_terms(by_features(vector_sums)),
        ],
        axis=1,
    )
    pieces = jnp.pad(pieces, ((0, 0), (0, -pieces.shape[1] % 16), (0, 0)))
    arrived = exchange(pieces)
    at = [tokens, tokens + 3 * own_rows, tokens + 6 * own_rows, tokens + 6 * own_rows + 3 * count]
    input_grad = jnp.sum(arrived[:, : at[0]].astype(F32), axis=0)
    input_grad = input_grad + from_terms(arrived[:, at[0] : at[1]]).reshape(tokens, features)
    output = from_terms(arrived[:, at[1] : at[2]]).reshape(tokens, features)
    vector_sums = jnp.sum(from_terms(arrived[:, at[2] : at[3]]), axis=0)

    first_section = section == 0
    kept = jnp.where(first_section, input_grad, output)
    other = section_swap(jnp.where(first_section, output, input_grad))
    own_first = batch == 0
    boundary = jnp.stack([jnp.where(own_first, kept, other), jnp.where(own_first, other, kept)])[None]

    hidden_size = hidden_bias.shape[0]
    return (
        boundary,
        qkv_grad[:, :HEAD],
        qkv_grad[:, HEAD : 2 * HEAD],
        qkv_grad[:, 2 * HEAD :],
        local_sums[hidden_size : hidden_size + HEAD],
        local_sums[hidden_size + HEAD :],
        out_grad,
        vector_sums[0],
        vector_sums[1],
        vector_sums[2],
        in_grad,
        local_sums[:hidden_size],
        down_grad,
        vector_sums[3],
        vector_sums[4],
        vector_sums[5],
    )


def solution(mesh):
    return jax.shard_map(
        body,
        mesh=mesh,
        in_specs=(
            P(None, "dp", "mp"),
            P(None, "dp", "mp"),
            P(),
            P("dp", "mp"),
            P("dp", "mp"),
            P("dp", "mp"),
            P("mp"),
            P("mp"),
            P("mp", "dp"),
            P("mp"),
            P("mp"),
            P("mp"),
            P("dp", "mp"),
            P("mp"),
            P("mp", "dp"),
            P("mp"),
            P("mp"),
            P("mp"),
        ),
        out_specs=(
            P("section", None, "dp", "mp"),
            P("dp", "mp"),
            P("dp", "mp"),
            P("dp", "mp"),
            P("mp"),
            P("mp"),
            P("mp", "dp"),
            P("mp"),
            P("mp"),
            P("mp"),
            P("dp", "mp"),
            P("mp"),
            P("mp", "dp"),
            P("mp"),
            P("mp"),
            P("mp"),
        ),
        check_vma=False,
    )
```

```python
import functools
import math

import jax
import jax.numpy as jnp
from jax import lax
from jax.experimental import pallas as pl
from jax.experimental.pallas import tpu as pltpu
from jax.sharding import PartitionSpec as P

HEAD = 128
SCALE = 1.0 / math.sqrt(HEAD)
EPS = 1e-06
BF = jnp.bfloat16
F32 = jnp.float32
STEPS = (0, 1, 3, 2)


def core_swap(array):
    count = lax.axis_size("dp")
    return lax.ppermute(array, "dp", [(i, i ^ 1) for i in range(count)])


def across(array, bits):
    count = lax.axis_size("dp")
    route = []
    for s in range(2):
        for i in range(count):
            x = (2 * (i // 2) + s) ^ bits
            route.append((s * count + i, (x % 2) * count + 2 * (x // 2) + i % 2))
    return lax.ppermute(array, ("section", "dp"), route)


def exchange(pieces):
    return lax.all_to_all(pieces, "mp", split_axis=0, concat_axis=0, tiled=True)


def after(array, *others):
    return lax.optimization_barrier((array, *others))[0]


def four_blocks(own, far):
    return own, core_swap(own), far, core_swap(far)


def split_terms(value):
    high = value.astype(BF)
    return high, (value - high.astype(F32)).astype(BF)


def dot(left, right):
    return jnp.dot(left, right, preferred_element_type=F32)


def dot_t(left, right):
    return lax.dot_general(left, right, (((1,), (1,)), ((), ())), preferred_element_type=F32)


def t_dot(left, right):
    return lax.dot_general(left, right, (((0,), (0,)), ((), ())), preferred_element_type=F32)


def gelu_tanh(value):
    inner = math.sqrt(2.0 / math.pi) * (value + 0.044715 * (value * value * value))
    bend = jnp.tanh(inner)
    slope = math.sqrt(2.0 / math.pi) * (1.0 + 3.0 * 0.044715 * (value * value))
    return 0.5 * value * (1.0 + bend), 0.5 * (1.0 + bend) + 0.5 * value * (1.0 - bend * bend) * slope


def call(kernel, outs, ids, *arrays):
    return pl.pallas_call(
        kernel,
        in_specs=[pl.BlockSpec(memory_space=pltpu.SMEM)] + [pl.BlockSpec(memory_space=pltpu.VMEM)] * len(arrays),
        out_specs=[pl.BlockSpec(memory_space=pltpu.VMEM)] * len(outs),
        out_shape=[jax.ShapeDtypeStruct(shape, dtype) for shape, dtype in outs],
        compiler_params=pltpu.CompilerParams(vmem_limit_bytes=40 * 2**20),
    )(ids, *arrays)


def columns_of(ids, k, width):
    return pl.ds(pl.multiple_of((ids[0] ^ k) * width, width), width)


def mask_of(ids, tokens, bits):
    def labels(place, shape, dim):
        places = place * tokens + lax.broadcasted_iota(jnp.int32, shape, dim)
        return sum((places >= ids[3 + j]).astype(jnp.int32) for j in range(4))

    return labels(ids[1], (tokens, 1), 0) == labels(ids[1] ^ bits, (1, tokens), 1)


def probabilities(ids, query, key_refs):
    scores = []
    for bits, ref in zip(STEPS, key_refs):
        same = mask_of(ids, query.shape[0], bits)
        scores.append(jnp.where(same, dot_t(query, ref[:, :HEAD]) * SCALE, -1e30))
    top = functools.reduce(jnp.maximum, [jnp.max(score, axis=-1, keepdims=True) for score in scores])
    expo = [jnp.exp(score - top) for score in scores]
    total = sum(jnp.sum(e, axis=-1, keepdims=True) for e in expo)
    return [e / total for e in expo]


def pack_kernel(own_rows, ids, own_input, other_input, own_cotangent, other_cotangent, vectors, pieces):
    core, same = ids[7], ids[7] == ids[8]
    parts, _, features = pieces.shape
    tokens = own_input.shape[1]
    values = jnp.where(same, own_input[core].astype(F32), other_input[core].astype(F32)).astype(BF)
    cotangent = jnp.where(same, own_cotangent[core], other_cotangent[core])
    vector_terms = jnp.concatenate(split_terms(vectors[...]), axis=0)
    for r in range(parts):
        pieces[r, :tokens, :] = values
        at = tokens
        for term in (*split_terms(cotangent[r * own_rows : (r + 1) * own_rows]), vector_terms):
            pieces[r, at : at + term.shape[0], :] = term
            at += term.shape[0]


def unpack_kernel(own_rows, ids, arrived, acts, rows, cotangent, vectors):
    parts, _, features = arrived.shape
    tokens = acts.shape[0]
    count = vectors.shape[0]
    for r in range(parts):
        columns = slice(r * features, (r + 1) * features)
        acts[:, columns] = arrived[r, :tokens, :]
        high, low, both = (
            arrived[r, tokens + k * own_rows : tokens + (k + 1) * own_rows, :].astype(F32) for k in range(3)
        )
        cotangent[:, columns] = high + low
        vectors[:, columns] = both[:count] + both[count:]
    rows[...] = acts[pl.ds(pl.multiple_of(ids[2] * own_rows, own_rows), own_rows), :].astype(F32)


def project_kernel(ids, acts, query_bias, pair_bias, *refs):
    weights, (query, pair) = refs[:-2], refs[-2:]
    total = 0.0
    for k in range(4):
        weight = jnp.concatenate([ref[...] for ref in weights[3 * k : 3 * k + 3]], axis=1)
        total = total + dot(acts[:, columns_of(ids, k, weight.shape[0])], weight)
    query[...] = (total[:, :HEAD] + query_bias[...]).astype(BF)
    pair[...] = (total[:, HEAD:] + pair_bias[...]).astype(BF)


def attend_kernel(ids, query, *refs):
    pairs, weights, (mixed, partial) = refs[:4], refs[4:8], refs[8:]
    probs = probabilities(ids, query[...], pairs)
    value = sum(dot(p.astype(BF), ref[:, HEAD:]) for p, ref in zip(probs, pairs)).astype(BF)
    mixed[...] = value
    for k, ref in enumerate(weights):
        partial[:, columns_of(ids, k, ref.shape[1])] = dot(value, ref[...]).astype(BF)


def hidden_kernel(ids, normed, bias, *refs):
    rising, falling, (inner, active, partial) = refs[:4], refs[4:8], refs[8:]
    total = bias[...]
    for k, ref in enumerate(rising):
        total = total + dot(normed[:, columns_of(ids, k, ref.shape[0])], ref[...])
    inner[...] = total
    value = gelu_tanh(total)[0].astype(BF)
    active[...] = value
    for k, ref in enumerate(falling):
        partial[:, columns_of(ids, k, ref.shape[1])] = dot(value, ref[...]).astype(BF)


def hidden_back_kernel(ids, grad, inner, *refs):
    rising, falling, (inner_grad, bias_grad, partial) = refs[:4], refs[4:8], refs[8:]
    total = 0.0
    for k, ref in enumerate(falling):
        total = total + dot_t(grad[:, columns_of(ids, k, ref.shape[1])], ref[...])
    value = (total * gelu_tanh(inner[...])[1]).astype(BF)
    inner_grad[...] = value
    bias_grad[...] = jnp.sum(value.astype(F32), axis=0, keepdims=True)
    for k, ref in enumerate(rising):
        partial[:, columns_of(ids, k, ref.shape[0])] = dot_t(value, ref[...]).astype(BF)


def attend_back_kernel(ids, grad, query, *refs):
    pairs, weights, (query_grad, own, *sent) = refs[:4], refs[4:8], refs[8:]
    mixed_grad = 0.0
    for k, ref in enumerate(weights):
        mixed_grad = mixed_grad + dot_t(grad[:, columns_of(ids, k, ref.shape[1])], ref[...])
    mixed_grad = mixed_grad.astype(BF)
    probs = probabilities(ids, query[...], pairs)
    prob_grads = [dot_t(mixed_grad, ref[:, HEAD:]) for ref in pairs]
    inside = sum(jnp.sum(p * g, axis=-1, keepdims=True) for p, g in zip(probs, prob_grads))
    score_grads = [(p * (g - inside)).astype(BF) for p, g in zip(probs, prob_grads)]
    query_grad[...] = (sum(dot(s, ref[:, :HEAD]) for s, ref in zip(score_grads, pairs)) * SCALE).astype(BF)
    for s, p, ref in zip(score_grads, probs, (own, *sent)):
        ref[:, :HEAD] = (t_dot(s, query[...]) * SCALE).astype(ref.dtype)
        ref[:, HEAD:] = t_dot(p.astype(BF), mixed_grad).astype(ref.dtype)


def joined_grads(query_grad, own, arrived, qkv_grad, bias_grad):
    pair = own[...]
    for ref in arrived:
        pair = pair + ref[...].astype(F32)
    value = jnp.concatenate([query_grad[...], pair.astype(BF)], axis=1)
    qkv_grad[...] = value
    bias_grad[...] = jnp.sum(value.astype(F32), axis=0, keepdims=True)
    return value


def project_back_kernel(ids, query_grad, own, *refs):
    arrived, weights, (qkv_grad, bias_grad, partial) = refs[:3], refs[3:15], refs[15:]
    value = joined_grads(query_grad, own, arrived, qkv_grad, bias_grad)
    for k in range(4):
        weight = jnp.concatenate([ref[...] for ref in weights[3 * k : 3 * k + 3]], axis=1)
        partial[:, columns_of(ids, k, weight.shape[0])] = dot_t(value, weight).astype(BF)


def last_back_kernel(ids, query_grad, own, *refs):
    arrived, weights, (grad, last_rows), vector_refs = refs[:3], refs[3:15], refs[15:17], refs[17:21]
    qkv_grad, bias_grad, pieces = refs[21:]
    value = joined_grads(query_grad, own, arrived, qkv_grad, bias_grad)
    tokens, own_rows = value.shape[0], grad.shape[0]
    row = lax.broadcasted_iota(jnp.int32, (tokens, 1), 0) // own_rows
    for k in range(4):
        weight = jnp.concatenate([ref[...] for ref in weights[3 * k : 3 * k + 3]], axis=1)
        block = dot_t(value, weight)
        own_block = grad[:, columns_of(ids, k, weight.shape[0])]
        repeated = jnp.concatenate([own_block] * (tokens // own_rows), axis=0)
        block = jnp.where(row == ids[2], block + repeated, block).astype(BF)
        for j in range(weight.shape[0] // HEAD):
            pieces[(ids[0] ^ k) * (weight.shape[0] // HEAD) + j, :tokens, :] = block[:, j * HEAD : (j + 1) * HEAD]
    for r in range(pieces.shape[0]):
        columns = slice(r * HEAD, (r + 1) * HEAD)
        high, low = split_terms(last_rows[:, columns])
        pieces[r, tokens : tokens + own_rows, :] = high
        pieces[r, tokens + own_rows : tokens + 2 * own_rows, :] = low
        terms = split_terms(sum(ref[:, columns] for ref in vector_refs))
        pieces[r, tokens + 2 * own_rows : tokens + 2 * own_rows + 16, :] = jnp.concatenate(terms, axis=0)


def norm_of(value, gain, shift):
    mean = jnp.mean(value, axis=-1, keepdims=True)
    centered = value - mean
    rstd = lax.rsqrt(jnp.mean(centered * centered, axis=-1, keepdims=True) + EPS)
    standard = centered * rstd
    return standard * gain + shift, standard, rstd


def norm_back(grad, standard, rstd, gain):
    scaled = grad * gain
    mean = jnp.mean(scaled, axis=-1, keepdims=True)
    cross = jnp.mean(scaled * standard, axis=-1, keepdims=True)
    return rstd * (scaled - mean - standard * cross)


def to_all(copies, value):
    low = value.astype(BF)
    for r in range(copies.shape[0]):
        copies[r] = low


def summed(arrived):
    total = arrived[0].astype(F32)
    for r in range(1, arrived.shape[0]):
        total = total + arrived[r].astype(F32)
    return total


def column_sums(first, grad, standard, back):
    row = lax.broadcasted_iota(jnp.int32, (8, grad.shape[1]), 0)
    total = jnp.zeros((8, grad.shape[1]), F32)
    for k, value in enumerate((back, grad * standard, grad)):
        total = jnp.where(row == first + k, jnp.sum(value, axis=0, keepdims=True), total)
    return total


def norm_kernel(first, ids, arrived, residual, vectors, result, standard, rstd, copies):
    bias, gain, shift = (vectors[first + k : first + k + 1, :] for k in range(3))
    value, standard_rows, rstd_rows = norm_of(residual[...] + summed(arrived) + bias, gain, shift)
    to_all(copies, value)
    result[...], standard[...] = value, standard_rows
    rstd[...] = jnp.broadcast_to(rstd_rows, rstd.shape)


def norm_back_kernel(first, ids, arrived, residual, standard, rstd, vectors, back, sums, copies):
    grad = residual[...] + summed(arrived)
    value = norm_back(grad, standard[...], rstd[:, :1], vectors[first + 1 : first + 2, :])
    to_all(copies, value)
    back[...] = value
    sums[...] = column_sums(first, grad, standard[...], value)


def turn_kernel(ids, arrived, residual, cotangent, vectors, result, back, sums, copies):
    bias, gain, shift = (vectors[3 + k : 4 + k, :] for k in range(3))
    value, standard, rstd = norm_of(residual[...] + summed(arrived) + bias, gain, shift)
    result[...] = value
    grad = cotangent[...]
    value = norm_back(grad, standard, rstd, gain)
    to_all(copies, value)
    back[...] = value
    sums[...] = column_sums(3, grad, standard, value)


def meet_kernel(ids, arrived, both, vectors):
    parts, _, features = arrived.shape
    tokens = both.shape[1]
    own_rows = tokens // parts
    total, last = 0.0, 0.0
    for r in range(parts):
        total = total + arrived[r, :tokens, :].astype(F32)
        high, low, terms = (
            arrived[r, tokens + k * own_rows : tokens + (k + 1) * own_rows, :].astype(F32) for k in range(3)
        )
        both[1, r * own_rows : (r + 1) * own_rows, :] = high + low
        last = last + terms
    both[0] = total
    vectors[...] = last[:8] + last[8:]


def keep_kernel(ids, own, other, kept, sent):
    core, section = ids[7], ids[8]
    for ref, index in ((kept, section), (sent, 1 - section)):
        ref[core] = own[index]
        ref[1 - core] = other[index]


def weight_grads(ids, *products, base=()):
    tokens = products[0][1][0][0].shape[0]
    shapes = []
    for axis, pairs in products:
        shape = [pairs[0][0].shape[1], pairs[0][1].shape[1]]
        shape[axis] //= 4
        shapes.append(tuple(shape))
    stacked = len(shapes) > 1 and len(set(shapes)) == 1
    if base:
        whole_shape = base[0].shape[1:]
    elif stacked:
        whole_shape = (len(shapes), *shapes[0])
    else:
        whole_shape = (shapes[0][0], sum(shape[1] for shape in shapes))

    def kernel(ids, *refs):
        parts, at = [], 0
        for _, pairs in products:
            parts.append(sum(t_dot(refs[at + 2 * j][...], refs[at + 2 * j + 1][...]) for j in range(len(pairs))))
            at += 2 * len(pairs)

        def store(ref, earlier):
            if stacked:
                for j, part in enumerate(parts):
                    ref[0, j] = (part if earlier is None else part + earlier[0, j].astype(F32)).astype(BF)
            else:
                part = jnp.concatenate(parts, axis=1)
                width = part.shape[1]
                if earlier is not None:
                    part = part + earlier[0, :, :width].astype(F32)
                    if width < whole_shape[1]:
                        ref[0, :, width:] = earlier[0, :, width:]
                ref[0, :, :width] = part.astype(BF)

        earlier = refs[at : at + 2] if base else (None, None)
        pl.when(pl.program_id(0) < 2)(lambda: store(refs[-2], earlier[0]))
        pl.when(pl.program_id(0) >= 2)(lambda: store(refs[-1], earlier[1]))

    def cut(i, ids):
        return (0, ids[0] ^ jnp.where(i < 2, 2 * i + 1, 2 * i - 4))

    def whole(i, ids):
        return (0, 0)

    zeros = (0,) * len(whole_shape)
    specs = [
        pl.BlockSpec((tokens, shape[side]), cut if side == axis else whole)
        for (axis, pairs), shape in zip(products, shapes)
        for _ in pairs
        for side in range(2)
    ]
    shares = [
        pl.BlockSpec((1, *whole_shape), lambda i, ids: (jnp.minimum(i, 1), *zeros)),
        pl.BlockSpec((1, *whole_shape), lambda i, ids: (jnp.maximum(i - 2, 0), *zeros)),
    ]
    return pl.pallas_call(
        kernel,
        grid_spec=pltpu.PrefetchScalarGridSpec(
            num_scalar_prefetch=1,
            grid=(4,),
            in_specs=specs + (shares if base else []),
            out_specs=shares,
        ),
        out_shape=[jax.ShapeDtypeStruct((2, *whole_shape), BF)] * 2,
        compiler_params=pltpu.CompilerParams(vmem_limit_bytes=40 * 2**20),
    )(ids, *[array for _, pairs in products for pair in pairs for array in pair], *base)


def add(left, right):
    return (left.astype(F32) + right.astype(F32)).astype(BF)


def core_sums(sent, kept):
    total = add(kept, core_swap(sent))
    return total[0], total[1]


def body(
    layer_input,
    out_cotangent,
    doc_lengths,
    query_weight,
    key_weight,
    value_weight,
    query_bias,
    value_bias,
    output_weight,
    output_bias,
    attention_norm_gain,
    attention_norm_shift,
    hidden_weight,
    hidden_bias,
    proj_weight,
    proj_bias,
    closing_norm_gain,
    closing_norm_shift,
):
    section = lax.axis_index("section")
    part = lax.axis_index("dp")
    place = lax.axis_index("mp")
    parts = lax.axis_size("mp")
    core = part % 2
    x = 2 * (part // 2) + section
    tokens, features = layer_input.shape[1:]
    own_rows = tokens // parts

    other_input, other_cotangent = core_swap(layer_input), core_swap(out_cotangent)

    qkv_far = [across(array, 3) for array in (query_weight, key_weight, value_weight)]
    out_far = across(output_weight, 3)
    qkv_blocks = [four_blocks(own, far) for own, far in zip((query_weight, key_weight, value_weight), qkv_far)]
    qkv_weights = [array for block in zip(*qkv_blocks) for array in block]
    out_weights = four_blocks(output_weight, out_far)
    hidden_core = core_swap(hidden_weight), core_swap(proj_weight)

    vectors = jnp.stack(
        [output_bias, attention_norm_gain, attention_norm_shift, proj_bias, closing_norm_gain, closing_norm_shift]
    )
    bounds = jnp.cumsum(lax.dynamic_index_in_dim(doc_lengths, core, 0, keepdims=False)).astype(jnp.int32)
    ids = jnp.concatenate([jnp.stack([part, x, place]).astype(jnp.int32), bounds, jnp.stack([core, section]).astype(jnp.int32)])

    (arrived,) = call(
        functools.partial(pack_kernel, own_rows),
        (((parts, tokens + 2 * own_rows + 16, features), BF),),
        ids,
        layer_input,
        other_input,
        out_cotangent,
        other_cotangent,
        jnp.pad(vectors, ((0, 2), (0, 0))),
    )
    arrived = after(exchange(arrived), *hidden_core)

    width = parts * features
    full, some = ((tokens, width), BF), ((own_rows, width), F32)
    copies = ((parts, own_rows, width), BF)
    eight = ((8, width), F32)
    narrow = ((own_rows, HEAD), F32)
    pair_shape = (tokens, 2 * HEAD)
    hidden_size = hidden_bias.shape[0]

    def cut_rows(partial):
        return partial.reshape(parts, own_rows, width)

    def whole(stack):
        return stack.reshape(tokens, width)

    acts_one, rows, cotangent, vectors = call(
        functools.partial(unpack_kernel, own_rows), (full, some, some, eight), ids, arrived
    )
    query_bias_row = query_bias[None]
    pair_bias_row = jnp.concatenate([jnp.zeros_like(value_bias), value_bias])[None]
    hidden_bias_row = hidden_bias[None]

    def keys_of(acts):
        query, pair = call(
            project_kernel,
            (((tokens, HEAD), BF), (pair_shape, BF)),
            ids,
            acts,
            query_bias_row,
            pair_bias_row,
            *qkv_weights,
        )
        return query, [pair] + [across(pair, bits) for bits in STEPS[1:]]

    def forward(query, pairs, residual, weights_then):
        mixed, partial = call(
            attend_kernel, (((tokens, HEAD), BF), full), ids, query, *pairs, *out_weights
        )
        arrived = exchange(cut_rows(partial))
        normed, standard, rstd, normed_copies = call(
            functools.partial(norm_kernel, 0), (some, some, narrow, copies), ids, arrived, residual, vectors
        )
        normed_copies, weights = weights_then(normed_copies, arrived)
        normed_full = whole(exchange(normed_copies))
        inner, active, partial = call(
            hidden_kernel,
            (((tokens, hidden_size), F32), ((tokens, hidden_size), BF), full),
            ids,
            normed_full,
            hidden_bias_row,
            *weights,
        )
        return exchange(cut_rows(partial)), normed, (mixed, standard, rstd, normed_full, inner, active)

    def backward_hidden(grad, grad_full, kept, weights, beside=lambda partial, inner_grad: partial):
        _, standard, rstd, _, inner, _ = kept
        inner_grad, bias_grad, partial = call(
            hidden_back_kernel,
            (((tokens, hidden_size), BF), ((1, hidden_size), F32), full),
            ids,
            grad_full,
            inner,
            *weights,
        )
        arrived = exchange(cut_rows(beside(partial, inner_grad)))
        back, sums, back_copies = call(
            functools.partial(norm_back_kernel, 0),
            (some, eight, copies),
            ids,
            arrived,
            grad,
            standard,
            rstd,
            vectors,
        )
        return back, sums, back_copies, inner_grad, bias_grad

    def backward_attention(grad_full, query, pairs):
        query_grad, own, *sent = call(
            attend_back_kernel,
            (((tokens, HEAD), BF), (pair_shape, F32), *[(pair_shape, BF)] * 3),
            ids,
            grad_full,
            query,
            *pairs,
            *out_weights,
        )
        return query_grad, own, [across(array, bits) for array, bits in zip(sent, STEPS[1:])]

    query_one, pairs_one = keys_of(acts_one)
    hidden_own = (hidden_weight, proj_weight)
    hidden_far = across(after(jnp.stack(hidden_own), *pairs_one), 3)
    hidden_weights = []

    def set_out(normed_copies, arrived):
        far = after(hidden_far, arrived)
        far = (far[0], far[1])
        far_core = [core_swap(array) for array in far]
        for j in range(2):
            hidden_weights.extend((hidden_own[j], hidden_core[j], far[j], far_core[j]))
        return after(normed_copies, *far_core), hidden_weights

    arrived, normed_one, kept_one = forward(query_one, pairs_one, rows, set_out)
    middle_rows, standard_one, rstd_one, row_copies = call(
        functools.partial(norm_kernel, 3), (some, some, narrow, copies), ids, arrived, normed_one, vectors
    )
    acts_two = whole(exchange(row_copies))
    query_two, pairs_two = keys_of(acts_two)
    arrived, normed_two, kept_two = forward(
        query_two, pairs_two, middle_rows, lambda normed_copies, arrived: (normed_copies, hidden_weights)
    )
    last_rows, grad, sums_a, grad_copies = call(
        turn_kernel, (some, some, eight, copies), ids, arrived, normed_two, cotangent, vectors
    )

    two_full = whole(exchange(grad_copies))
    grad, sums_b, grad_copies, inner_grad_two, hidden_bias_two = backward_hidden(grad, two_full, kept_two, hidden_weights)
    one_full = whole(exchange(grad_copies))
    query_grad, own, sent = backward_attention(one_full, query_two, pairs_two)
    hidden_base = weight_grads(
        after(ids, query_grad), (0, ((kept_two[3], inner_grad_two),)), (1, ((kept_two[5], two_full),))
    )
    own = after(own, *hidden_base)
    qkv_grad_two, bias_grad_two, partial = call(
        project_back_kernel,
        (((tokens, 3 * HEAD), BF), ((1, 3 * HEAD), F32), full),
        ids,
        query_grad,
        own,
        *sent,
        *qkv_weights,
    )
    arrived = exchange(cut_rows(partial))
    grad, sums_c, grad_copies = call(
        functools.partial(norm_back_kernel, 3), (some, eight, copies), ids, arrived, grad, standard_one, rstd_one, vectors
    )

    two_full_one = whole(exchange(grad_copies))
    hidden_sums = []

    def hidden_shares(partial, inner_grad):
        products = ((0, ((kept_one[3], inner_grad),)), (1, ((kept_one[5], two_full_one),)))
        hidden_sums.extend(core_sums(*weight_grads(ids, *products, base=hidden_base)))
        return after(partial, *hidden_sums)

    grad, sums_d, grad_copies, inner_grad_one, hidden_bias_one = backward_hidden(
        grad, two_full_one, kept_one, hidden_weights, hidden_shares
    )
    hidden_near = add(hidden_sums[0], across(hidden_sums[1], 3))
    one_full_one = whole(exchange(grad_copies))
    query_grad, own, sent = backward_attention(one_full_one, query_one, pairs_one)
    attention_base = weight_grads(
        after(ids, query_grad),
        (0, ((acts_two, qkv_grad_two),)),
        (0, ((one_full, kept_two[0]), (one_full_one, kept_one[0]))),
    )
    own = after(own, hidden_near, *attention_base)

    qkv_grad_one, bias_grad_one, pieces = call(
        last_back_kernel,
        (((tokens, 3 * HEAD), BF), ((1, 3 * HEAD), F32), ((parts, tokens + 2 * own_rows + 16, features), BF)),
        ids,
        query_grad,
        own,
        *sent,
        *qkv_weights,
        grad,
        last_rows,
        sums_a,
        sums_b,
        sums_c,
        sums_d,
    )
    near, far = core_sums(*weight_grads(ids, (0, ((acts_one, qkv_grad_one),)), base=attention_base))
    arrived = exchange(after(pieces, near, far))
    near = add(near, across(far, 3))
    attention_last = across(near, 1)
    hidden_sum = hidden_near.astype(F32) + across(hidden_near, 1).astype(F32)

    two = ((2, tokens, features), F32)
    own, vector_sums = call(meet_kernel, (two, ((8, features), F32)), ids, arrived)
    kept, sent = call(keep_kernel, (two, two), ids, own, core_swap(own))
    count = lax.axis_size("dp")
    route = [(s * count + i, (1 - s) * count + i) for s in range(2) for i in range(count) if i % 2 == s]
    passed = lax.ppermute(sent, ("section", "dp"), route)
    attention_sum = near.astype(F32) + after(attention_last, passed).astype(F32)
    boundary = jnp.where(core == section, kept, passed)[None]

    bias_grads = (bias_grad_two + bias_grad_one)[0]
    small = jnp.concatenate([(hidden_bias_two + hidden_bias_one)[0], bias_grads, vector_sums.reshape(-1)])
    small = small + core_swap(small)
    small = small + across(after(small, sent), 3)
    small = small + across(small, 1)
    bias_at = hidden_size + 3 * HEAD
    vector_sums = small[bias_at:].reshape(8, features)

    return (
        boundary,
        attention_sum[:, :HEAD],
        attention_sum[:, HEAD : 2 * HEAD],
        attention_sum[:, 2 * HEAD : 3 * HEAD],
        small[hidden_size : hidden_size + HEAD],
        small[hidden_size + 2 * HEAD : bias_at],
        attention_sum[:, 3 * HEAD :].T,
        vector_sums[0],
        vector_sums[1],
        vector_sums[2],
        hidden_sum[0],
        small[:hidden_size],
        hidden_sum[1],
        vector_sums[3],
        vector_sums[4],
        vector_sums[5],
    )


def solution(mesh):
    return jax.shard_map(
        body,
        mesh=mesh,
        in_specs=(
            P(None, "dp", "mp"),
            P(None, "dp", "mp"),
            P(),
            P("dp", "mp"),
            P("dp", "mp"),
            P("dp", "mp"),
            P("mp"),
            P("mp"),
            P("mp", "dp"),
            P("mp"),
            P("mp"),
            P("mp"),
            P("dp", "mp"),
            P("mp"),
            P("mp", "dp"),
            P("mp"),
            P("mp"),
            P("mp"),
        ),
        out_specs=(
            P("section", None, "dp", "mp"),
            P("dp", "mp"),
            P("dp", "mp"),
            P("dp", "mp"),
            P("mp"),
            P("mp"),
            P("mp", "dp"),
            P("mp"),
            P("mp"),
            P("mp"),
            P("dp", "mp"),
            P("mp"),
            P("mp", "dp"),
            P("mp"),
            P("mp"),
            P("mp"),
        ),
        check_vma=False,
    )
```

```python
import functools
import math

import jax
import jax.numpy as jnp
from jax import lax
from jax.experimental import pallas as pl
from jax.experimental.pallas import tpu as pltpu
from jax.sharding import PartitionSpec as P

HEAD = 128
SCALE = 1.0 / math.sqrt(HEAD)
EPS = 1e-06
BF = jnp.bfloat16
F32 = jnp.float32
STEPS = (0, 1, 3, 2)


def core_swap(array):
    count = lax.axis_size("dp")
    return lax.ppermute(array, "dp", [(i, i ^ 1) for i in range(count)])


def across(array, bits):
    count = lax.axis_size("dp")
    route = []
    for s in range(2):
        for i in range(count):
            x = (2 * (i // 2) + s) ^ bits
            route.append((s * count + i, (x % 2) * count + 2 * (x // 2) + i % 2))
    return lax.ppermute(array, ("section", "dp"), route)


def exchange(pieces):
    return lax.all_to_all(pieces, "mp", split_axis=0, concat_axis=0, tiled=True)


def after(array, *others):
    return lax.optimization_barrier((array, *others))[0]


def four_blocks(own, far):
    return own, core_swap(own), far, core_swap(far)


def split_terms(value):
    high = value.astype(BF)
    return high, (value - high.astype(F32)).astype(BF)


def dot(left, right):
    return jnp.dot(left, right, preferred_element_type=F32)


def dot_t(left, right):
    return lax.dot_general(left, right, (((1,), (1,)), ((), ())), preferred_element_type=F32)


def t_dot(left, right):
    return lax.dot_general(left, right, (((0,), (0,)), ((), ())), preferred_element_type=F32)


def gelu_tanh(value):
    inner = math.sqrt(2.0 / math.pi) * (value + 0.044715 * (value * value * value))
    bend = jnp.tanh(inner)
    slope = math.sqrt(2.0 / math.pi) * (1.0 + 3.0 * 0.044715 * (value * value))
    return 0.5 * value * (1.0 + bend), 0.5 * (1.0 + bend) + 0.5 * value * (1.0 - bend * bend) * slope


def call(kernel, outs, ids, *arrays, behind=()):
    count = len(arrays)

    def body(ids, *refs):
        kernel(ids, *refs[:count], *refs[count + len(behind) :])

    in_specs = [pl.BlockSpec(memory_space=pltpu.SMEM)] + [pl.BlockSpec(memory_space=pltpu.VMEM)] * count
    return pl.pallas_call(
        body,
        in_specs=in_specs + [pl.BlockSpec(memory_space=pl.ANY)] * len(behind),
        out_specs=[pl.BlockSpec(memory_space=pltpu.VMEM)] * len(outs),
        out_shape=[jax.ShapeDtypeStruct(shape, dtype) for shape, dtype in outs],
        compiler_params=pltpu.CompilerParams(vmem_limit_bytes=40 * 2**20),
    )(ids, *arrays, *behind)


def gate(array, *behind):
    return pl.pallas_call(
        lambda *refs: None,
        in_specs=[pl.BlockSpec(memory_space=pl.ANY)] * (1 + len(behind)),
        out_specs=pl.BlockSpec(memory_space=pl.ANY),
        out_shape=jax.ShapeDtypeStruct(array.shape, array.dtype),
        input_output_aliases={0: 0},
    )(array, *behind)


def columns_of(ids, k, width):
    return pl.ds(pl.multiple_of((ids[0] ^ k) * width, width), width)


def mask_of(ids, tokens, bits):
    def labels(place, shape, dim):
        places = place * tokens + lax.broadcasted_iota(jnp.int32, shape, dim)
        return sum((places >= ids[3 + j]).astype(jnp.int32) for j in range(4))

    return labels(ids[1], (tokens, 1), 0) == labels(ids[1] ^ bits, (1, tokens), 1)


def probabilities(ids, query, key_refs):
    scores = []
    for bits, ref in zip(STEPS, key_refs):
        same = mask_of(ids, query.shape[0], bits)
        scores.append(jnp.where(same, dot_t(query, ref[:, :HEAD]) * SCALE, -1e30))
    top = functools.reduce(jnp.maximum, [jnp.max(score, axis=-1, keepdims=True) for score in scores])
    expo = [jnp.exp(score - top) for score in scores]
    total = sum(jnp.sum(e, axis=-1, keepdims=True) for e in expo)
    return [e / total for e in expo]


def pack_kernel(own_rows, ids, own_input, other_input, own_cotangent, other_cotangent, vectors, pieces):
    core, same = ids[7], ids[7] == ids[8]
    parts, _, features = pieces.shape
    tokens = own_input.shape[1]
    values = jnp.where(same, own_input[core].astype(F32), other_input[core].astype(F32)).astype(BF)
    cotangent = jnp.where(same, own_cotangent[core], other_cotangent[core])
    vector_terms = jnp.concatenate(split_terms(vectors[...]), axis=0)
    for r in range(parts):
        pieces[r, :tokens, :] = values
        at = tokens
        for term in (*split_terms(cotangent[r * own_rows : (r + 1) * own_rows]), vector_terms):
            pieces[r, at : at + term.shape[0], :] = term
            at += term.shape[0]


def unpack_kernel(own_rows, ids, arrived, acts, rows, cotangent, vectors):
    parts, _, features = arrived.shape
    tokens = acts.shape[0]
    count = vectors.shape[0]
    for r in range(parts):
        columns = slice(r * features, (r + 1) * features)
        acts[:, columns] = arrived[r, :tokens, :]
        high, low, both = (
            arrived[r, tokens + k * own_rows : tokens + (k + 1) * own_rows, :].astype(F32) for k in range(3)
        )
        cotangent[:, columns] = high + low
        vectors[:, columns] = both[:count] + both[count:]
    rows[...] = acts[pl.ds(pl.multiple_of(ids[2] * own_rows, own_rows), own_rows), :].astype(F32)


def bundle_kernel(ids, *refs):
    bundle = refs[-1]
    for k in range(4):
        for j in range(3):
            bundle[k, :, j * HEAD : (j + 1) * HEAD] = refs[3 * k + j][...]


def project_kernel(ids, acts, query_bias, pair_bias, weights, query, pair):
    total = 0.0
    for k in range(4):
        total = total + dot(acts[:, columns_of(ids, k, weights.shape[1])], weights[k])
    query[...] = (total[:, :HEAD] + query_bias[...]).astype(BF)
    pair[...] = (total[:, HEAD:] + pair_bias[...]).astype(BF)


def attend_kernel(ids, query, *refs):
    pairs, weights, (mixed, partial, bundle) = refs[:4], refs[4], refs[5:]
    for k, ref in enumerate(pairs):
        bundle[k] = ref[...]
    probs = probabilities(ids, query[...], pairs)
    value = sum(dot(p.astype(BF), ref[:, HEAD:]) for p, ref in zip(probs, pairs)).astype(BF)
    mixed[...] = value
    for k in range(4):
        partial[:, columns_of(ids, k, weights.shape[2])] = dot(value, weights[k]).astype(BF)


def hidden_kernel(ids, normed, bias, *refs):
    rising, falling, (inner, active, partial) = refs[:4], refs[4:8], refs[8:]
    total = bias[...]
    for k, ref in enumerate(rising):
        total = total + dot(normed[:, columns_of(ids, k, ref.shape[0])], ref[...])
    inner[...] = total
    value = gelu_tanh(total)[0].astype(BF)
    active[...] = value
    for k, ref in enumerate(falling):
        partial[:, columns_of(ids, k, ref.shape[1])] = dot(value, ref[...]).astype(BF)


def hidden_back_kernel(ids, grad, inner, *refs):
    rising, falling, (inner_grad, bias_grad, partial) = refs[:4], refs[4:8], refs[8:]
    total = 0.0
    for k, ref in enumerate(falling):
        total = total + dot_t(grad[:, columns_of(ids, k, ref.shape[1])], ref[...])
    value = (total * gelu_tanh(inner[...])[1]).astype(BF)
    inner_grad[...] = value
    bias_grad[...] = jnp.sum(value.astype(F32), axis=0, keepdims=True)
    for k, ref in enumerate(rising):
        partial[:, columns_of(ids, k, ref.shape[0])] = dot_t(value, ref[...]).astype(BF)


def attend_back_kernel(ids, grad, query, bundle, weights, query_grad, own, *sent):
    pairs = [bundle.at[k] for k in range(4)]
    mixed_grad = 0.0
    for k in range(4):
        mixed_grad = mixed_grad + dot_t(grad[:, columns_of(ids, k, weights.shape[2])], weights[k])
    mixed_grad = mixed_grad.astype(BF)
    probs = probabilities(ids, query[...], pairs)
    prob_grads = [dot_t(mixed_grad, ref[:, HEAD:]) for ref in pairs]
    inside = sum(jnp.sum(p * g, axis=-1, keepdims=True) for p, g in zip(probs, prob_grads))
    score_grads = [(p * (g - inside)).astype(BF) for p, g in zip(probs, prob_grads)]
    query_grad[...] = (sum(dot(s, ref[:, :HEAD]) for s, ref in zip(score_grads, pairs)) * SCALE).astype(BF)
    for s, p, ref in zip(score_grads, probs, (own, *sent)):
        ref[:, :HEAD] = (t_dot(s, query[...]) * SCALE).astype(ref.dtype)
        ref[:, HEAD:] = t_dot(p.astype(BF), mixed_grad).astype(ref.dtype)


def joined_grads(query_grad, own, arrived, qkv_grad, bias_grad):
    pair = own[...]
    for ref in arrived:
        pair = pair + ref[...].astype(F32)
    value = jnp.concatenate([query_grad[...], pair.astype(BF)], axis=1)
    qkv_grad[...] = value
    bias_grad[...] = jnp.sum(value.astype(F32), axis=0, keepdims=True)
    return value


def project_back_kernel(ids, query_grad, own, *refs):
    arrived, weights, (qkv_grad, bias_grad, partial) = refs[:3], refs[3], refs[4:]
    value = joined_grads(query_grad, own, arrived, qkv_grad, bias_grad)
    for k in range(4):
        partial[:, columns_of(ids, k, weights.shape[1])] = dot_t(value, weights[k]).astype(BF)


def last_back_kernel(ids, query_grad, own, *refs):
    arrived, weights, (grad, last_rows), vector_refs = refs[:3], refs[3], refs[4:6], refs[6:10]
    qkv_grad, bias_grad, pieces = refs[10:]
    value = joined_grads(query_grad, own, arrived, qkv_grad, bias_grad)
    tokens, own_rows = value.shape[0], grad.shape[0]
    row = lax.broadcasted_iota(jnp.int32, (tokens, 1), 0) // own_rows
    for k in range(4):
        weight = weights[k]
        block = dot_t(value, weight)
        own_block = grad[:, columns_of(ids, k, weight.shape[0])]
        repeated = jnp.concatenate([own_block] * (tokens // own_rows), axis=0)
        block = jnp.where(row == ids[2], block + repeated, block).astype(BF)
        for j in range(weight.shape[0] // HEAD):
            pieces[(ids[0] ^ k) * (weight.shape[0] // HEAD) + j, :tokens, :] = block[:, j * HEAD : (j + 1) * HEAD]
    for r in range(pieces.shape[0]):
        columns = slice(r * HEAD, (r + 1) * HEAD)
        high, low = split_terms(last_rows[:, columns])
        pieces[r, tokens : tokens + own_rows, :] = high
        pieces[r, tokens + own_rows : tokens + 2 * own_rows, :] = low
        terms = split_terms(sum(ref[:, columns] for ref in vector_refs))
        pieces[r, tokens + 2 * own_rows : tokens + 2 * own_rows + 16, :] = jnp.concatenate(terms, axis=0)


def norm_of(value, gain, shift):
    mean = jnp.mean(value, axis=-1, keepdims=True)
    centered = value - mean
    rstd = lax.rsqrt(jnp.mean(centered * centered, axis=-1, keepdims=True) + EPS)
    standard = centered * rstd
    return standard * gain + shift, standard, rstd


def norm_back(grad, standard, rstd, gain):
    scaled = grad * gain
    mean = jnp.mean(scaled, axis=-1, keepdims=True)
    cross = jnp.mean(scaled * standard, axis=-1, keepdims=True)
    return rstd * (scaled - mean - standard * cross)


def to_all(copies, value):
    low = value.astype(BF)
    for r in range(copies.shape[0]):
        copies[r] = low


def summed(arrived):
    total = arrived[0].astype(F32)
    for r in range(1, arrived.shape[0]):
        total = total + arrived[r].astype(F32)
    return total


def column_sums(first, grad, standard, back):
    row = lax.broadcasted_iota(jnp.int32, (8, grad.shape[1]), 0)
    total = jnp.zeros((8, grad.shape[1]), F32)
    for k, value in enumerate((back, grad * standard, grad)):
        total = jnp.where(row == first + k, jnp.sum(value, axis=0, keepdims=True), total)
    return total


def norm_kernel(first, ids, arrived, residual, vectors, result, standard, rstd, copies):
    bias, gain, shift = (vectors[first + k : first + k + 1, :] for k in range(3))
    value, standard_rows, rstd_rows = norm_of(residual[...] + summed(arrived) + bias, gain, shift)
    to_all(copies, value)
    result[...], standard[...] = value, standard_rows
    rstd[...] = jnp.broadcast_to(rstd_rows, rstd.shape)


def norm_back_kernel(first, ids, arrived, residual, standard, rstd, vectors, back, sums, copies):
    grad = residual[...] + summed(arrived)
    value = norm_back(grad, standard[...], rstd[:, :1], vectors[first + 1 : first + 2, :])
    to_all(copies, value)
    back[...] = value
    sums[...] = column_sums(first, grad, standard[...], value)


def norm_back_and_sums_kernel(first, ids, arrived, residual, standard, rstd, vectors, kept, swapped, *outs):
    norm_back_kernel(first, ids, arrived, residual, standard, rstd, vectors, *outs[:3])
    core_sums_kernel(ids, kept, swapped, *outs[3:])


def turn_kernel(ids, arrived, residual, cotangent, vectors, result, back, sums, copies):
    bias, gain, shift = (vectors[3 + k : 4 + k, :] for k in range(3))
    value, standard, rstd = norm_of(residual[...] + summed(arrived) + bias, gain, shift)
    result[...] = value
    grad = cotangent[...]
    value = norm_back(grad, standard, rstd, gain)
    to_all(copies, value)
    back[...] = value
    sums[...] = column_sums(3, grad, standard, value)


def meet_kernel(ids, arrived, both, vectors):
    parts, _, features = arrived.shape
    tokens = both.shape[1]
    own_rows = tokens // parts
    total, last = 0.0, 0.0
    for r in range(parts):
        total = total + arrived[r, :tokens, :].astype(F32)
        high, low, terms = (
            arrived[r, tokens + k * own_rows : tokens + (k + 1) * own_rows, :].astype(F32) for k in range(3)
        )
        both[1, r * own_rows : (r + 1) * own_rows, :] = high + low
        last = last + terms
    both[0] = total
    vectors[...] = last[:8] + last[8:]


def keep_kernel(ids, own, other, own_small, other_small, kept, sent):
    core, section = ids[7], ids[8]
    tokens = own.shape[1]
    rows = own_small.shape[0]
    total = own_small[...] + other_small[...]
    kept[2 * tokens :, :] = total
    sent[2 * tokens :, :] = total
    for ref, index in ((kept, section), (sent, 1 - section)):
        ref[pl.ds(pl.multiple_of(core * tokens, tokens), tokens), :] = own[index]
        ref[pl.ds(pl.multiple_of((1 - core) * tokens, tokens), tokens), :] = other[index]


def weight_grads(ids, *products, base=(), behind=()):
    tokens = products[0][1][0][0].shape[0]
    shapes = []
    for axis, pairs in products:
        shape = [pairs[0][0].shape[1], pairs[0][1].shape[1]]
        shape[axis] //= 4
        shapes.append(tuple(shape))
    stacked = len(shapes) > 1 and len(set(shapes)) == 1
    if base:
        whole_shape = base[0].shape[1:]
    elif stacked:
        whole_shape = (len(shapes), *shapes[0])
    else:
        whole_shape = (shapes[0][0], sum(shape[1] for shape in shapes))

    def kernel(ids, *refs):
        parts, at = [], 0
        for _, pairs in products:
            parts.append(sum(t_dot(refs[at + 2 * j][...], refs[at + 2 * j + 1][...]) for j in range(len(pairs))))
            at += 2 * len(pairs)

        def store(ref, earlier):
            if stacked:
                for j, part in enumerate(parts):
                    ref[0, j] = (part if earlier is None else part + earlier[0, j].astype(F32)).astype(BF)
            else:
                part = jnp.concatenate(parts, axis=1)
                width = part.shape[1]
                if earlier is not None:
                    part = part + earlier[0, :, :width].astype(F32)
                    if width < whole_shape[1]:
                        ref[0, :, width:] = earlier[0, :, width:]
                ref[0, :, :width] = part.astype(BF)

        earlier = refs[at : at + 2] if base else (None, None)
        pl.when(pl.program_id(0) < 2)(lambda: store(refs[-2], earlier[0]))
        pl.when(pl.program_id(0) >= 2)(lambda: store(refs[-1], earlier[1]))

    def cut(i, ids):
        return (0, ids[0] ^ jnp.where(i < 2, 2 * i + 1, 2 * i - 4))

    def whole(i, ids):
        return (0, 0)

    zeros = (0,) * len(whole_shape)
    specs = [
        pl.BlockSpec((tokens, shape[side]), cut if side == axis else whole)
        for (axis, pairs), shape in zip(products, shapes)
        for _ in pairs
        for side in range(2)
    ]
    shares = [
        pl.BlockSpec((1, *whole_shape), lambda i, ids: (jnp.minimum(i, 1), *zeros)),
        pl.BlockSpec((1, *whole_shape), lambda i, ids: (jnp.maximum(i - 2, 0), *zeros)),
    ]
    return pl.pallas_call(
        kernel,
        grid_spec=pltpu.PrefetchScalarGridSpec(
            num_scalar_prefetch=1,
            grid=(4,),
            in_specs=specs + (shares if base else []) + [pl.BlockSpec(memory_space=pl.ANY)] * len(behind),
            out_specs=shares,
        ),
        out_shape=[jax.ShapeDtypeStruct((2, *whole_shape), BF)] * 2,
        compiler_params=pltpu.CompilerParams(vmem_limit_bytes=40 * 2**20),
    )(ids, *[array for _, pairs in products for pair in pairs for array in pair], *base, *behind)


def add_kernel(ids, left, right, total):
    total[...] = (left[...].astype(F32) + right[...].astype(F32)).astype(total.dtype)


def hidden_sums(left, right, behind):
    _, rows, columns = left.shape

    def kernel(left, right, _, first, second, held, leaving):
        copies = []
        for j, ref in enumerate((first, second)):
            held[j] = left[j].astype(F32) + right[j].astype(F32)
            copies.append(pltpu.make_async_copy(held.at[j], ref, leaving.at[j]))
            copies[j].start()
        for copy in copies:
            copy.wait()

    return pl.pallas_call(
        kernel,
        in_specs=[pl.BlockSpec(memory_space=pltpu.VMEM)] * 2 + [pl.BlockSpec(memory_space=pl.ANY)],
        out_specs=[pl.BlockSpec(memory_space=pltpu.HBM)] * 2,
        out_shape=[jax.ShapeDtypeStruct((rows, columns), F32)] * 2,
        scratch_shapes=[pltpu.VMEM(left.shape, F32), pltpu.SemaphoreType.DMA((2,))],
        compiler_params=pltpu.CompilerParams(vmem_limit_bytes=40 * 2**20),
    )(left, right, behind)


def core_sums_kernel(ids, kept, arrived, near, far):
    for j, ref in enumerate((near, far)):
        ref[...] = (kept[j].astype(F32) + arrived[j].astype(F32)).astype(BF)


def last_sums_kernel(ids, left, right, query, key, value, out):
    for j, ref in enumerate((query, key, value)):
        columns = slice(j * HEAD, (j + 1) * HEAD)
        ref[...] = left[:, columns].astype(F32) + right[:, columns].astype(F32)
    out[...] = (left[:, 3 * HEAD :].astype(F32) + right[:, 3 * HEAD :].astype(F32)).T


def body(
    layer_input,
    out_cotangent,
    doc_lengths,
    query_weight,
    key_weight,
    value_weight,
    query_bias,
    value_bias,
    output_weight,
    output_bias,
    attention_norm_gain,
    attention_norm_shift,
    hidden_weight,
    hidden_bias,
    proj_weight,
    proj_bias,
    closing_norm_gain,
    closing_norm_shift,
):
    section = lax.axis_index("section")
    part = lax.axis_index("dp")
    place = lax.axis_index("mp")
    parts = lax.axis_size("mp")
    core = part % 2
    x = 2 * (part // 2) + section
    tokens, features = layer_input.shape[1:]
    own_rows = tokens // parts

    other_input, other_cotangent = core_swap(layer_input), core_swap(out_cotangent)

    qkv_far = [across(array, 3) for array in (query_weight, key_weight, value_weight)]
    out_far = across(output_weight, 3)
    qkv_blocks = [four_blocks(own, far) for own, far in zip((query_weight, key_weight, value_weight), qkv_far)]
    qkv_weights = [array for block in zip(*qkv_blocks) for array in block]
    out_weights = jnp.stack(four_blocks(output_weight, out_far))
    hidden_core = core_swap(hidden_weight), core_swap(proj_weight)

    vectors = jnp.stack(
        [output_bias, attention_norm_gain, attention_norm_shift, proj_bias, closing_norm_gain, closing_norm_shift]
    )
    bounds = jnp.cumsum(lax.dynamic_index_in_dim(doc_lengths, core, 0, keepdims=False)).astype(jnp.int32)
    ids = jnp.concatenate([jnp.stack([part, x, place]).astype(jnp.int32), bounds, jnp.stack([core, section]).astype(jnp.int32)])

    (arrived,) = call(
        functools.partial(pack_kernel, own_rows),
        (((parts, tokens + 2 * own_rows + 16, features), BF),),
        ids,
        layer_input,
        other_input,
        out_cotangent,
        other_cotangent,
        jnp.pad(vectors, ((0, 2), (0, 0))),
    )
    arrived = after(exchange(arrived), *hidden_core)

    width = parts * features
    full, some = ((tokens, width), BF), ((own_rows, width), F32)
    copies = ((parts, own_rows, width), BF)
    eight = ((8, width), F32)
    narrow = ((own_rows, HEAD), F32)
    pair_shape = (tokens, 2 * HEAD)
    hidden_size = hidden_bias.shape[0]

    block = ((hidden_size, hidden_size), BF)
    full_block = ((hidden_size, hidden_size), F32)
    blocks = ((2, hidden_size, hidden_size), BF)

    def cut_rows(partial):
        return partial.reshape(parts, own_rows, width)

    def whole(stack):
        return stack.reshape(tokens, width)

    hidden_own = (hidden_weight, proj_weight)
    hidden_stack = jnp.stack(hidden_own)
    (qkv_weights,) = call(bundle_kernel, (((4, 4 * HEAD, 3 * HEAD), BF),), ids, *qkv_weights)
    acts_one, rows, cotangent, vectors = call(
        functools.partial(unpack_kernel, own_rows), (full, some, some, eight), ids, arrived, behind=(hidden_stack,)
    )
    query_bias_row = query_bias[None]
    pair_bias_row = jnp.concatenate([jnp.zeros_like(value_bias), value_bias])[None]
    hidden_bias_row = hidden_bias[None]

    def keys_of(acts):
        query, pair = call(
            project_kernel,
            (((tokens, HEAD), BF), (pair_shape, BF)),
            ids,
            acts,
            query_bias_row,
            pair_bias_row,
            qkv_weights,
        )
        return query, [pair] + [across(pair, bits) for bits in STEPS[1:]]

    def forward(query, pairs, residual, weights_then):
        mixed, partial, bundle = call(
            attend_kernel,
            (((tokens, HEAD), BF), full, ((4, *pair_shape), BF)),
            ids,
            query,
            *pairs,
            out_weights,
        )
        arrived = exchange(cut_rows(partial))
        normed, standard, rstd, normed_copies = call(
            functools.partial(norm_kernel, 0), (some, some, narrow, copies), ids, arrived, residual, vectors
        )
        normed_copies, weights = weights_then(normed_copies, arrived)
        normed_full = whole(exchange(normed_copies))
        inner, active, partial = call(
            hidden_kernel,
            (((tokens, hidden_size), F32), ((tokens, hidden_size), BF), full),
            ids,
            normed_full,
            hidden_bias_row,
            *weights,
        )
        return exchange(cut_rows(partial)), normed, (mixed, standard, rstd, normed_full, inner, active), bundle

    def backward_hidden(grad, grad_full, kept, weights, beside=lambda inner_grad: ()):
        _, standard, rstd, _, inner, _ = kept
        inner_grad, bias_grad, partial = call(
            hidden_back_kernel,
            (((tokens, hidden_size), BF), ((1, hidden_size), F32), full),
            ids,
            grad_full,
            inner,
            *weights,
        )
        arrived = exchange(cut_rows(partial))
        shares = beside(inner_grad)
        back, sums, back_copies, *core_sums = call(
            functools.partial(norm_back_and_sums_kernel if shares else norm_back_kernel, 0),
            (some, eight, copies, *[blocks] * len(shares)),
            ids,
            arrived,
            grad,
            standard,
            rstd,
            vectors,
            *shares,
        )
        return back, sums, back_copies, inner_grad, bias_grad, *core_sums

    def backward_attention(grad_full, query, bundle, behind=()):
        query_grad, own, *sent = call(
            attend_back_kernel,
            (((tokens, HEAD), BF), (pair_shape, F32), *[(pair_shape, BF)] * 3),
            ids,
            grad_full,
            query,
            bundle,
            out_weights,
            behind=behind,
        )
        return query_grad, own, [across(array, bits) for array, bits in zip(sent, STEPS[1:])]

    query_one, pairs_one = keys_of(acts_one)
    hidden_far = across(hidden_stack, 3)
    hidden_weights = []

    def set_out(normed_copies, arrived):
        far = after(hidden_far, arrived)
        far = (far[0], far[1])
        far_core = [core_swap(array) for array in far]
        for j in range(2):
            hidden_weights.extend((hidden_own[j], hidden_core[j], far[j], far_core[j]))
        return after(normed_copies, *far_core), hidden_weights

    arrived, normed_one, kept_one, bundle_one = forward(query_one, pairs_one, rows, set_out)
    middle_rows, standard_one, rstd_one, row_copies = call(
        functools.partial(norm_kernel, 3), (some, some, narrow, copies), ids, arrived, normed_one, vectors
    )
    acts_two = whole(exchange(row_copies))
    query_two, pairs_two = keys_of(acts_two)
    arrived, normed_two, kept_two, bundle_two = forward(
        query_two, pairs_two, middle_rows, lambda normed_copies, arrived: (normed_copies, hidden_weights)
    )
    last_rows, grad, sums_a, grad_copies = call(
        turn_kernel, (some, some, eight, copies), ids, arrived, normed_two, cotangent, vectors
    )

    two_full = whole(exchange(grad_copies))
    grad, sums_b, grad_copies, inner_grad_two, hidden_bias_two = backward_hidden(grad, two_full, kept_two, hidden_weights)
    one_full = whole(exchange(grad_copies))
    query_grad, own, sent = backward_attention(one_full, query_two, bundle_two)
    hidden_base = weight_grads(
        ids, (0, ((kept_two[3], inner_grad_two),)), (1, ((kept_two[5], two_full),)), behind=sent[:1]
    )
    qkv_grad_two, bias_grad_two, partial = call(
        project_back_kernel,
        (((tokens, 3 * HEAD), BF), ((1, 3 * HEAD), F32), full),
        ids,
        query_grad,
        own,
        *sent,
        qkv_weights,
        behind=hidden_base[:1],
    )
    arrived = exchange(cut_rows(partial))
    grad, sums_c, grad_copies = call(
        functools.partial(norm_back_kernel, 3), (some, eight, copies), ids, arrived, grad, standard_one, rstd_one, vectors
    )

    two_full_one = whole(exchange(grad_copies))

    def hidden_shares(inner_grad):
        sent, kept = weight_grads(
            ids, (0, ((kept_one[3], inner_grad),)), (1, ((kept_one[5], two_full_one),)), base=hidden_base
        )
        return kept, core_swap(sent)

    grad, sums_d, grad_copies, inner_grad_one, hidden_bias_one, hidden_near, hidden_far = backward_hidden(
        grad, two_full_one, kept_one, hidden_weights, hidden_shares
    )
    hidden_far = across(hidden_far, 3)
    one_full_one = whole(exchange(grad_copies))
    query_grad, own, sent = backward_attention(one_full_one, query_one, bundle_one)
    (hidden_near,) = call(add_kernel, (blocks,), ids, hidden_near, hidden_far, behind=sent[:1])
    hidden_last = across(hidden_near, 1)
    attention_base = weight_grads(
        ids,
        (0, ((acts_two, qkv_grad_two),)),
        (0, ((one_full, kept_two[0]), (one_full_one, kept_one[0]))),
        behind=sent[:1],
    )

    qkv_grad_one, bias_grad_one, pieces = call(
        last_back_kernel,
        (((tokens, 3 * HEAD), BF), ((1, 3 * HEAD), F32), ((parts, tokens + 2 * own_rows + 16, features), BF)),
        ids,
        query_grad,
        own,
        *sent,
        qkv_weights,
        grad,
        last_rows,
        sums_a,
        sums_b,
        sums_c,
        sums_d,
        behind=attention_base[:1],
    )
    arrived = exchange(pieces)

    sent, kept = weight_grads(ids, (0, ((acts_one, qkv_grad_one),)), base=attention_base)
    near, far = call(core_sums_kernel, (block, block), ids, kept, core_swap(sent))
    near_sum, far_sum = near, far
    (near,) = call(add_kernel, (block,), ids, near, across(far, 3))

    two = ((2, tokens, features), F32)
    own, vector_sums = call(meet_kernel, (two, ((8, features), F32)), ids, arrived, behind=(far_sum,))
    bias_grads = (bias_grad_two + bias_grad_one)[0]
    small = jnp.concatenate([(hidden_bias_two + hidden_bias_one)[0], bias_grads, vector_sums.reshape(-1)])
    small = jnp.pad(small, (0, -small.shape[0] % (8 * features))).reshape(-1, features)
    rows_out = ((2 * tokens + small.shape[0], features), F32)
    kept, sent = call(keep_kernel, (rows_out, rows_out), ids, own, core_swap(own), small, core_swap(small))
    passed = across(sent, 1)
    small = kept[2 * tokens :] + passed[2 * tokens :]
    small = (small + across(small, 3)).reshape(-1)
    bias_at = hidden_size + 3 * HEAD
    vector_sums = small[bias_at : bias_at + 8 * features].reshape(8, features)
    boundary = jnp.where(core == section, kept[: 2 * tokens], passed[: 2 * tokens]).reshape(1, 2, tokens, features)

    attention_last = across(near, 1)
    in_sum, down_sum = hidden_sums(hidden_near, hidden_last, sent)
    square, wide = ((hidden_size, HEAD), F32), ((HEAD, hidden_size), F32)
    query_sum, key_sum, value_sum, out_sum = call(
        last_sums_kernel, (square, square, square, wide), ids, near, attention_last, behind=(in_sum, down_sum)
    )

    return (
        boundary,
        query_sum,
        key_sum,
        value_sum,
        small[hidden_size : hidden_size + HEAD],
        small[hidden_size + 2 * HEAD : bias_at],
        out_sum,
        vector_sums[0],
        vector_sums[1],
        vector_sums[2],
        in_sum,
        small[:hidden_size],
        down_sum,
        vector_sums[3],
        vector_sums[4],
        vector_sums[5],
    )


def solution(mesh):
    return jax.shard_map(
        body,
        mesh=mesh,
        in_specs=(
            P(None, "dp", "mp"),
            P(None, "dp", "mp"),
            P(),
            P("dp", "mp"),
            P("dp", "mp"),
            P("dp", "mp"),
            P("mp"),
            P("mp"),
            P("mp", "dp"),
            P("mp"),
            P("mp"),
            P("mp"),
            P("dp", "mp"),
            P("mp"),
            P("mp", "dp"),
            P("mp"),
            P("mp"),
            P("mp"),
        ),
        out_specs=(
            P("section", None, "dp", "mp"),
            P("dp", "mp"),
            P("dp", "mp"),
            P("dp", "mp"),
            P("mp"),
            P("mp"),
            P("mp", "dp"),
            P("mp"),
            P("mp"),
            P("mp"),
            P("dp", "mp"),
            P("mp"),
            P("mp", "dp"),
            P("mp"),
            P("mp"),
            P("mp"),
        ),
        check_vma=False,
    )
```

```python
import functools
import math

import jax
import jax.numpy as jnp
from jax import lax
from jax.experimental import pallas as pl
from jax.experimental.pallas import tpu as pltpu
from jax.sharding import PartitionSpec as P

HEAD = 128
SCALE = 1.0 / math.sqrt(HEAD)
EPS = 1e-06
BF = jnp.bfloat16
F32 = jnp.float32
STEPS = (0, 1, 3, 2)


def core_swap(array):
    count = lax.axis_size("dp")
    return lax.ppermute(array, "dp", [(i, i ^ 1) for i in range(count)])


def across(array, bits):
    count = lax.axis_size("dp")
    route = []
    for s in range(2):
        for i in range(count):
            x = (2 * (i // 2) + s) ^ bits
            route.append((s * count + i, (x % 2) * count + 2 * (x // 2) + i % 2))
    return lax.ppermute(array, ("section", "dp"), route)


def exchange(pieces):
    return lax.all_to_all(pieces, "mp", split_axis=0, concat_axis=0, tiled=True)


def after(array, *others):
    return lax.optimization_barrier((array, *others))[0]


def four_blocks(own, far):
    return own, core_swap(own), far, core_swap(far)


def split_terms(value):
    high = value.astype(BF)
    return high, (value - high.astype(F32)).astype(BF)


def dot(left, right):
    return jnp.dot(left, right, preferred_element_type=F32)


def dot_t(left, right):
    return lax.dot_general(left, right, (((1,), (1,)), ((), ())), preferred_element_type=F32)


def t_dot(left, right):
    return lax.dot_general(left, right, (((0,), (0,)), ((), ())), preferred_element_type=F32)


def gelu_tanh(value):
    inner = math.sqrt(2.0 / math.pi) * (value + 0.044715 * (value * value * value))
    bend = jnp.tanh(inner)
    slope = math.sqrt(2.0 / math.pi) * (1.0 + 3.0 * 0.044715 * (value * value))
    return 0.5 * value * (1.0 + bend), 0.5 * (1.0 + bend) + 0.5 * value * (1.0 - bend * bend) * slope


def call(kernel, outs, ids, *arrays, behind=()):
    count = len(arrays)

    def body(ids, *refs):
        kernel(ids, *refs[:count], *refs[count + len(behind) :])

    in_specs = [pl.BlockSpec(memory_space=pltpu.SMEM)] + [pl.BlockSpec(memory_space=pltpu.VMEM)] * count
    return pl.pallas_call(
        body,
        in_specs=in_specs + [pl.BlockSpec(memory_space=pl.ANY)] * len(behind),
        out_specs=[pl.BlockSpec(memory_space=pltpu.VMEM)] * len(outs),
        out_shape=[jax.ShapeDtypeStruct(shape, dtype) for shape, dtype in outs],
        compiler_params=pltpu.CompilerParams(vmem_limit_bytes=40 * 2**20),
    )(ids, *arrays, *behind)


def gate(array, *behind):
    return pl.pallas_call(
        lambda *refs: None,
        in_specs=[pl.BlockSpec(memory_space=pl.ANY)] * (1 + len(behind)),
        out_specs=pl.BlockSpec(memory_space=pl.ANY),
        out_shape=jax.ShapeDtypeStruct(array.shape, array.dtype),
        input_output_aliases={0: 0},
    )(array, *behind)


def columns_of(ids, k, width):
    return pl.ds(pl.multiple_of((ids[0] ^ k) * width, width), width)


def mask_of(ids, tokens, bits):
    def labels(place, shape, dim):
        places = place * tokens + lax.broadcasted_iota(jnp.int32, shape, dim)
        return sum((places >= ids[3 + j]).astype(jnp.int32) for j in range(4))

    return labels(ids[1], (tokens, 1), 0) == labels(ids[1] ^ bits, (1, tokens), 1)


def probabilities(ids, query, key_refs):
    scores = []
    for bits, ref in zip(STEPS, key_refs):
        same = mask_of(ids, query.shape[0], bits)
        scores.append(jnp.where(same, dot_t(query, ref[:, :HEAD]) * SCALE, -1e30))
    top = functools.reduce(jnp.maximum, [jnp.max(score, axis=-1, keepdims=True) for score in scores])
    expo = [jnp.exp(score - top) for score in scores]
    total = sum(jnp.sum(e, axis=-1, keepdims=True) for e in expo)
    return [e / total for e in expo]


def pack_kernel(own_rows, ids, own_input, other_input, own_cotangent, other_cotangent, vectors, pieces):
    core, same = ids[7], ids[7] == ids[8]
    parts, _, features = pieces.shape
    tokens = own_input.shape[1]
    values = jnp.where(same, own_input[core].astype(F32), other_input[core].astype(F32)).astype(BF)
    cotangent = jnp.where(same, own_cotangent[core], other_cotangent[core])
    vector_terms = jnp.concatenate(split_terms(vectors[...]), axis=0)
    for r in range(parts):
        pieces[r, :tokens, :] = values
        at = tokens
        for term in (*split_terms(cotangent[r * own_rows : (r + 1) * own_rows]), vector_terms):
            pieces[r, at : at + term.shape[0], :] = term
            at += term.shape[0]


def unpack_kernel(own_rows, ids, arrived, acts, rows, cotangent, vectors):
    parts, _, features = arrived.shape
    tokens = acts.shape[0]
    count = vectors.shape[0]
    for r in range(parts):
        columns = slice(r * features, (r + 1) * features)
        acts[:, columns] = arrived[r, :tokens, :]
        high, low, both = (
            arrived[r, tokens + k * own_rows : tokens + (k + 1) * own_rows, :].astype(F32) for k in range(3)
        )
        cotangent[:, columns] = high + low
        vectors[:, columns] = both[:count] + both[count:]
    rows[...] = acts[pl.ds(pl.multiple_of(ids[2] * own_rows, own_rows), own_rows), :].astype(F32)


def bundle_kernel(ids, *refs):
    bundle = refs[-1]
    for k in range(4):
        for j in range(3):
            bundle[k, :, j * HEAD : (j + 1) * HEAD] = refs[3 * k + j][...]


def project_kernel(ids, acts, query_bias, pair_bias, weights, query, pair):
    total = 0.0
    for k in range(4):
        total = total + dot(acts[:, columns_of(ids, k, weights.shape[1])], weights[k])
    query[...] = (total[:, :HEAD] + query_bias[...]).astype(BF)
    pair[...] = (total[:, HEAD:] + pair_bias[...]).astype(BF)


def attend_kernel(ids, query, *refs):
    pairs, weights, (mixed, partial, bundle) = refs[:4], refs[4], refs[5:]
    for k, ref in enumerate(pairs):
        bundle[k] = ref[...]
    probs = probabilities(ids, query[...], pairs)
    value = sum(dot(p.astype(BF), ref[:, HEAD:]) for p, ref in zip(probs, pairs)).astype(BF)
    mixed[...] = value
    for k in range(4):
        partial[:, columns_of(ids, k, weights.shape[2])] = dot(value, weights[k]).astype(BF)


def hidden_kernel(ids, normed, bias, *refs):
    rising, falling, (inner, active, partial) = refs[:4], refs[4:8], refs[8:]
    total = bias[...]
    for k, ref in enumerate(rising):
        total = total + dot(normed[:, columns_of(ids, k, ref.shape[0])], ref[...])
    inner[...] = total
    value = gelu_tanh(total)[0].astype(BF)
    active[...] = value
    for k, ref in enumerate(falling):
        partial[:, columns_of(ids, k, ref.shape[1])] = dot(value, ref[...]).astype(BF)


def hidden_back_kernel(ids, grad, inner, *refs):
    rising, falling, (inner_grad, bias_grad, partial) = refs[:4], refs[4:8], refs[8:]
    total = 0.0
    for k, ref in enumerate(falling):
        total = total + dot_t(grad[:, columns_of(ids, k, ref.shape[1])], ref[...])
    value = (total * gelu_tanh(inner[...])[1]).astype(BF)
    inner_grad[...] = value
    bias_grad[...] = jnp.sum(value.astype(F32), axis=0, keepdims=True)
    for k, ref in enumerate(rising):
        partial[:, columns_of(ids, k, ref.shape[0])] = dot_t(value, ref[...]).astype(BF)


def attend_back_kernel(ids, grad, query, bundle, weights, query_grad, own, *sent):
    pairs = [bundle.at[k] for k in range(4)]
    mixed_grad = 0.0
    for k in range(4):
        mixed_grad = mixed_grad + dot_t(grad[:, columns_of(ids, k, weights.shape[2])], weights[k])
    mixed_grad = mixed_grad.astype(BF)
    probs = probabilities(ids, query[...], pairs)
    prob_grads = [dot_t(mixed_grad, ref[:, HEAD:]) for ref in pairs]
    inside = sum(jnp.sum(p * g, axis=-1, keepdims=True) for p, g in zip(probs, prob_grads))
    score_grads = [(p * (g - inside)).astype(BF) for p, g in zip(probs, prob_grads)]
    query_grad[...] = (sum(dot(s, ref[:, :HEAD]) for s, ref in zip(score_grads, pairs)) * SCALE).astype(BF)
    for s, p, ref in zip(score_grads, probs, (own, *sent)):
        ref[:, :HEAD] = (t_dot(s, query[...]) * SCALE).astype(ref.dtype)
        ref[:, HEAD:] = t_dot(p.astype(BF), mixed_grad).astype(ref.dtype)


def joined_grads(query_grad, own, arrived, qkv_grad, bias_grad):
    pair = own[...]
    for ref in arrived:
        pair = pair + ref[...].astype(F32)
    value = jnp.concatenate([query_grad[...], pair.astype(BF)], axis=1)
    qkv_grad[...] = value
    bias_grad[...] = jnp.sum(value.astype(F32), axis=0, keepdims=True)
    return value


def project_back_kernel(ids, query_grad, own, *refs):
    arrived, weights, (qkv_grad, bias_grad, partial) = refs[:3], refs[3], refs[4:]
    value = joined_grads(query_grad, own, arrived, qkv_grad, bias_grad)
    for k in range(4):
        partial[:, columns_of(ids, k, weights.shape[1])] = dot_t(value, weights[k]).astype(BF)


def last_back_kernel(ids, query_grad, own, *refs):
    arrived, weights, (grad, last_rows), vector_refs = refs[:3], refs[3], refs[4:6], refs[6:10]
    qkv_grad, bias_grad, pieces = refs[10:]
    value = joined_grads(query_grad, own, arrived, qkv_grad, bias_grad)
    tokens, own_rows = value.shape[0], grad.shape[0]
    row = lax.broadcasted_iota(jnp.int32, (tokens, 1), 0) // own_rows
    for k in range(4):
        weight = weights[k]
        block = dot_t(value, weight)
        own_block = grad[:, columns_of(ids, k, weight.shape[0])]
        repeated = jnp.concatenate([own_block] * (tokens // own_rows), axis=0)
        block = jnp.where(row == ids[2], block + repeated, block).astype(BF)
        for j in range(weight.shape[0] // HEAD):
            pieces[(ids[0] ^ k) * (weight.shape[0] // HEAD) + j, :tokens, :] = block[:, j * HEAD : (j + 1) * HEAD]
    for r in range(pieces.shape[0]):
        columns = slice(r * HEAD, (r + 1) * HEAD)
        high, low = split_terms(last_rows[:, columns])
        pieces[r, tokens : tokens + own_rows, :] = high
        pieces[r, tokens + own_rows : tokens + 2 * own_rows, :] = low
        terms = split_terms(sum(ref[:, columns] for ref in vector_refs))
        pieces[r, tokens + 2 * own_rows : tokens + 2 * own_rows + 16, :] = jnp.concatenate(terms, axis=0)


def norm_of(value, gain, shift):
    mean = jnp.mean(value, axis=-1, keepdims=True)
    centered = value - mean
    rstd = lax.rsqrt(jnp.mean(centered * centered, axis=-1, keepdims=True) + EPS)
    standard = centered * rstd
    return standard * gain + shift, standard, rstd


def norm_back(grad, standard, rstd, gain):
    scaled = grad * gain
    mean = jnp.mean(scaled, axis=-1, keepdims=True)
    cross = jnp.mean(scaled * standard, axis=-1, keepdims=True)
    return rstd * (scaled - mean - standard * cross)


def to_all(copies, value):
    low = value.astype(BF)
    for r in range(copies.shape[0]):
        copies[r] = low


def summed(arrived):
    total = arrived[0].astype(F32)
    for r in range(1, arrived.shape[0]):
        total = total + arrived[r].astype(F32)
    return total


def column_sums(first, grad, standard, back):
    row = lax.broadcasted_iota(jnp.int32, (8, grad.shape[1]), 0)
    total = jnp.zeros((8, grad.shape[1]), F32)
    for k, value in enumerate((back, grad * standard, grad)):
        total = jnp.where(row == first + k, jnp.sum(value, axis=0, keepdims=True), total)
    return total


def norm_kernel(first, ids, arrived, residual, vectors, result, standard, rstd, copies):
    bias, gain, shift = (vectors[first + k : first + k + 1, :] for k in range(3))
    value, standard_rows, rstd_rows = norm_of(residual[...] + summed(arrived) + bias, gain, shift)
    to_all(copies, value)
    result[...], standard[...] = value, standard_rows
    rstd[...] = jnp.broadcast_to(rstd_rows, rstd.shape)


def norm_back_kernel(first, ids, arrived, residual, standard, rstd, vectors, back, sums, copies):
    grad = residual[...] + summed(arrived)
    value = norm_back(grad, standard[...], rstd[:, :1], vectors[first + 1 : first + 2, :])
    to_all(copies, value)
    back[...] = value
    sums[...] = column_sums(first, grad, standard[...], value)


def norm_back_and_sums_kernel(first, ids, arrived, residual, standard, rstd, vectors, kept, swapped, *outs):
    norm_back_kernel(first, ids, arrived, residual, standard, rstd, vectors, *outs[:3])
    core_sums_kernel(ids, kept, swapped, *outs[3:])


def turn_kernel(ids, arrived, residual, cotangent, vectors, result, back, sums, copies):
    bias, gain, shift = (vectors[3 + k : 4 + k, :] for k in range(3))
    value, standard, rstd = norm_of(residual[...] + summed(arrived) + bias, gain, shift)
    result[...] = value
    grad = cotangent[...]
    value = norm_back(grad, standard, rstd, gain)
    to_all(copies, value)
    back[...] = value
    sums[...] = column_sums(3, grad, standard, value)


def meet_kernel(ids, arrived, both, vectors):
    parts, _, features = arrived.shape
    tokens = both.shape[1]
    own_rows = tokens // parts
    total, last = 0.0, 0.0
    for r in range(parts):
        total = total + arrived[r, :tokens, :].astype(F32)
        high, low, terms = (
            arrived[r, tokens + k * own_rows : tokens + (k + 1) * own_rows, :].astype(F32) for k in range(3)
        )
        both[1, r * own_rows : (r + 1) * own_rows, :] = high + low
        last = last + terms
    both[0] = total
    vectors[...] = last[:8] + last[8:]


def keep_kernel(ids, own, other, own_small, other_small, kept, sent):
    core, section = ids[7], ids[8]
    tokens = own.shape[1]
    rows = own_small.shape[0]
    total = own_small[...] + other_small[...]
    kept[2 * tokens :, :] = total
    sent[2 * tokens :, :] = total
    for ref, index in ((kept, section), (sent, 1 - section)):
        ref[pl.ds(pl.multiple_of(core * tokens, tokens), tokens), :] = own[index]
        ref[pl.ds(pl.multiple_of((1 - core) * tokens, tokens), tokens), :] = other[index]


def weight_grads(ids, *products, base=(), behind=(), far_first=False):
    tokens = products[0][1][0][0].shape[0]
    shapes = []
    for axis, pairs in products:
        shape = [pairs[0][0].shape[1], pairs[0][1].shape[1]]
        shape[axis] //= 4
        shapes.append(tuple(shape))
    stacked = len(shapes) > 1 and len(set(shapes)) == 1
    if base:
        whole_shape = base[0].shape[1:]
    elif stacked:
        whole_shape = (len(shapes), *shapes[0])
    else:
        whole_shape = (shapes[0][0], sum(shape[1] for shape in shapes))

    def kernel(ids, *refs):
        parts, at = [], 0
        for _, pairs in products:
            parts.append(sum(t_dot(refs[at + 2 * j][...], refs[at + 2 * j + 1][...]) for j in range(len(pairs))))
            at += 2 * len(pairs)

        def store(ref, earlier):
            if stacked:
                for j, part in enumerate(parts):
                    ref[0, j] = (part if earlier is None else part + earlier[0, j].astype(F32)).astype(BF)
            else:
                part = jnp.concatenate(parts, axis=1)
                width = part.shape[1]
                if earlier is not None:
                    part = part + earlier[0, :, :width].astype(F32)
                    if width < whole_shape[1]:
                        ref[0, :, width:] = earlier[0, :, width:]
                ref[0, :, :width] = part.astype(BF)

        earlier = refs[at : at + 2] if base else (None, None)
        pl.when(pl.program_id(0) < 2)(lambda: store(refs[-2], earlier[0]))
        pl.when(pl.program_id(0) >= 2)(lambda: store(refs[-1], earlier[1]))

    def cut(i, ids):
        order = jnp.where(i < 2, i + 2, i - 2) if far_first else jnp.where(i < 2, 2 * i + 1, 2 * i - 4)
        return (0, ids[0] ^ order)

    def whole(i, ids):
        return (0, 0)

    zeros = (0,) * len(whole_shape)
    specs = [
        pl.BlockSpec((tokens, shape[side]), cut if side == axis else whole)
        for (axis, pairs), shape in zip(products, shapes)
        for _ in pairs
        for side in range(2)
    ]
    shares = [
        pl.BlockSpec((1, *whole_shape), lambda i, ids: (jnp.minimum(i, 1), *zeros)),
        pl.BlockSpec((1, *whole_shape), lambda i, ids: (jnp.maximum(i - 2, 0), *zeros)),
    ]
    return pl.pallas_call(
        kernel,
        grid_spec=pltpu.PrefetchScalarGridSpec(
            num_scalar_prefetch=1,
            grid=(4,),
            in_specs=specs + (shares if base else []) + [pl.BlockSpec(memory_space=pl.ANY)] * len(behind),
            out_specs=shares,
        ),
        out_shape=[jax.ShapeDtypeStruct((2, *whole_shape), BF)] * 2,
        compiler_params=pltpu.CompilerParams(vmem_limit_bytes=40 * 2**20),
    )(ids, *[array for _, pairs in products for pair in pairs for array in pair], *base, *behind)


def add_kernel(ids, left, right, total):
    total[...] = (left[...].astype(F32) + right[...].astype(F32)).astype(total.dtype)


def hidden_sums(left, right, behind):
    _, rows, columns = left.shape

    def kernel(left, right, _, first, second, held, leaving):
        copies = []
        for j, ref in enumerate((first, second)):
            held[j] = left[j].astype(F32) + right[j].astype(F32)
            copies.append(pltpu.make_async_copy(held.at[j], ref, leaving.at[j]))
            copies[j].start()
        for copy in copies:
            copy.wait()

    return pl.pallas_call(
        kernel,
        in_specs=[pl.BlockSpec(memory_space=pltpu.VMEM)] * 2 + [pl.BlockSpec(memory_space=pl.ANY)],
        out_specs=[pl.BlockSpec(memory_space=pltpu.HBM)] * 2,
        out_shape=[jax.ShapeDtypeStruct((rows, columns), F32)] * 2,
        scratch_shapes=[pltpu.VMEM(left.shape, F32), pltpu.SemaphoreType.DMA((2,))],
        compiler_params=pltpu.CompilerParams(vmem_limit_bytes=40 * 2**20),
    )(left, right, behind)


def core_sums_kernel(ids, kept, arrived, near, far):
    for j, ref in enumerate((near, far)):
        ref[...] = (kept[j].astype(F32) + arrived[j].astype(F32)).astype(BF)


def last_sums_kernel(ids, left, right, query, key, value, out):
    for j, ref in enumerate((query, key, value)):
        columns = slice(j * HEAD, (j + 1) * HEAD)
        ref[...] = left[:, columns].astype(F32) + right[:, columns].astype(F32)
    out[...] = (left[:, 3 * HEAD :].astype(F32) + right[:, 3 * HEAD :].astype(F32)).T


def body(
    layer_input,
    out_cotangent,
    doc_lengths,
    query_weight,
    key_weight,
    value_weight,
    query_bias,
    value_bias,
    output_weight,
    output_bias,
    attention_norm_gain,
    attention_norm_shift,
    hidden_weight,
    hidden_bias,
    proj_weight,
    proj_bias,
    closing_norm_gain,
    closing_norm_shift,
):
    section = lax.axis_index("section")
    part = lax.axis_index("dp")
    place = lax.axis_index("mp")
    parts = lax.axis_size("mp")
    core = part % 2
    x = 2 * (part // 2) + section
    tokens, features = layer_input.shape[1:]
    own_rows = tokens // parts

    other_input, other_cotangent = core_swap(layer_input), core_swap(out_cotangent)

    qkv_far = [across(array, 3) for array in (query_weight, key_weight, value_weight)]
    out_far = across(output_weight, 3)
    qkv_blocks = [four_blocks(own, far) for own, far in zip((query_weight, key_weight, value_weight), qkv_far)]
    qkv_weights = [array for block in zip(*qkv_blocks) for array in block]
    out_weights = jnp.stack(four_blocks(output_weight, out_far))
    hidden_core = core_swap(hidden_weight), core_swap(proj_weight)

    vectors = jnp.stack(
        [output_bias, attention_norm_gain, attention_norm_shift, proj_bias, closing_norm_gain, closing_norm_shift]
    )
    bounds = jnp.cumsum(lax.dynamic_index_in_dim(doc_lengths, core, 0, keepdims=False)).astype(jnp.int32)
    ids = jnp.concatenate([jnp.stack([part, x, place]).astype(jnp.int32), bounds, jnp.stack([core, section]).astype(jnp.int32)])

    (arrived,) = call(
        functools.partial(pack_kernel, own_rows),
        (((parts, tokens + 2 * own_rows + 16, features), BF),),
        ids,
        layer_input,
        other_input,
        out_cotangent,
        other_cotangent,
        jnp.pad(vectors, ((0, 2), (0, 0))),
    )
    arrived = after(exchange(arrived), *hidden_core)

    width = parts * features
    full, some = ((tokens, width), BF), ((own_rows, width), F32)
    copies = ((parts, own_rows, width), BF)
    eight = ((8, width), F32)
    narrow = ((own_rows, HEAD), F32)
    pair_shape = (tokens, 2 * HEAD)
    hidden_size = hidden_bias.shape[0]

    block = ((hidden_size, hidden_size), BF)
    full_block = ((hidden_size, hidden_size), F32)
    blocks = ((2, hidden_size, hidden_size), BF)

    def cut_rows(partial):
        return partial.reshape(parts, own_rows, width)

    def whole(stack):
        return stack.reshape(tokens, width)

    hidden_own = (hidden_weight, proj_weight)
    hidden_stack = jnp.stack(hidden_own)
    (qkv_weights,) = call(bundle_kernel, (((4, 4 * HEAD, 3 * HEAD), BF),), ids, *qkv_weights)
    acts_one, rows, cotangent, vectors = call(
        functools.partial(unpack_kernel, own_rows), (full, some, some, eight), ids, arrived, behind=(hidden_stack,)
    )
    query_bias_row = query_bias[None]
    pair_bias_row = jnp.concatenate([jnp.zeros_like(value_bias), value_bias])[None]
    hidden_bias_row = hidden_bias[None]

    def keys_of(acts):
        query, pair = call(
            project_kernel,
            (((tokens, HEAD), BF), (pair_shape, BF)),
            ids,
            acts,
            query_bias_row,
            pair_bias_row,
            qkv_weights,
        )
        return query, [pair] + [across(pair, bits) for bits in STEPS[1:]]

    def forward(query, pairs, residual, weights_then):
        mixed, partial, bundle = call(
            attend_kernel,
            (((tokens, HEAD), BF), full, ((4, *pair_shape), BF)),
            ids,
            query,
            *pairs,
            out_weights,
        )
        arrived = exchange(cut_rows(partial))
        normed, standard, rstd, normed_copies = call(
            functools.partial(norm_kernel, 0), (some, some, narrow, copies), ids, arrived, residual, vectors
        )
        normed_copies, weights = weights_then(normed_copies, arrived)
        normed_full = whole(exchange(normed_copies))
        inner, active, partial = call(
            hidden_kernel,
            (((tokens, hidden_size), F32), ((tokens, hidden_size), BF), full),
            ids,
            normed_full,
            hidden_bias_row,
            *weights,
        )
        return exchange(cut_rows(partial)), normed, (mixed, standard, rstd, normed_full, inner, active), bundle

    def backward_hidden(grad, grad_full, kept, weights, beside=lambda inner_grad: ()):
        _, standard, rstd, _, inner, _ = kept
        inner_grad, bias_grad, partial = call(
            hidden_back_kernel,
            (((tokens, hidden_size), BF), ((1, hidden_size), F32), full),
            ids,
            grad_full,
            inner,
            *weights,
        )
        arrived = exchange(cut_rows(partial))
        shares = beside(inner_grad)
        back, sums, back_copies, *core_sums = call(
            functools.partial(norm_back_and_sums_kernel if shares else norm_back_kernel, 0),
            (some, eight, copies, *[blocks] * len(shares)),
            ids,
            arrived,
            grad,
            standard,
            rstd,
            vectors,
            *shares,
        )
        return back, sums, back_copies, inner_grad, bias_grad, *core_sums

    def backward_attention(grad_full, query, bundle, behind=()):
        query_grad, own, *sent = call(
            attend_back_kernel,
            (((tokens, HEAD), BF), (pair_shape, F32), *[(pair_shape, BF)] * 3),
            ids,
            grad_full,
            query,
            bundle,
            out_weights,
            behind=behind,
        )
        return query_grad, own, [across(array, bits) for array, bits in zip(sent, STEPS[1:])]

    query_one, pairs_one = keys_of(acts_one)
    hidden_far = across(hidden_stack, 3)
    hidden_weights = []

    def set_out(normed_copies, arrived):
        far = after(hidden_far, arrived)
        far = (far[0], far[1])
        far_core = [core_swap(array) for array in far]
        for j in range(2):
            hidden_weights.extend((hidden_own[j], hidden_core[j], far[j], far_core[j]))
        return after(normed_copies, *far_core), hidden_weights

    arrived, normed_one, kept_one, bundle_one = forward(query_one, pairs_one, rows, set_out)
    middle_rows, standard_one, rstd_one, row_copies = call(
        functools.partial(norm_kernel, 3), (some, some, narrow, copies), ids, arrived, normed_one, vectors
    )
    acts_two = whole(exchange(row_copies))
    query_two, pairs_two = keys_of(acts_two)
    arrived, normed_two, kept_two, bundle_two = forward(
        query_two, pairs_two, middle_rows, lambda normed_copies, arrived: (normed_copies, hidden_weights)
    )
    last_rows, grad, sums_a, grad_copies = call(
        turn_kernel, (some, some, eight, copies), ids, arrived, normed_two, cotangent, vectors
    )

    two_full = whole(exchange(grad_copies))
    grad, sums_b, grad_copies, inner_grad_two, hidden_bias_two = backward_hidden(grad, two_full, kept_two, hidden_weights)
    one_full = whole(exchange(grad_copies))
    query_grad, own, sent = backward_attention(one_full, query_two, bundle_two)
    hidden_base = weight_grads(
        ids,
        (0, ((kept_two[3], inner_grad_two),)),
        (1, ((kept_two[5], two_full),)),
        behind=sent[:1],
        far_first=True,
    )
    qkv_grad_two, bias_grad_two, partial = call(
        project_back_kernel,
        (((tokens, 3 * HEAD), BF), ((1, 3 * HEAD), F32), full),
        ids,
        query_grad,
        own,
        *sent,
        qkv_weights,
        behind=hidden_base[:1],
    )
    arrived = exchange(cut_rows(partial))
    grad, sums_c, grad_copies = call(
        functools.partial(norm_back_kernel, 3), (some, eight, copies), ids, arrived, grad, standard_one, rstd_one, vectors
    )

    two_full_one = whole(exchange(grad_copies))
    grad, sums_d, grad_copies, inner_grad_one, hidden_bias_one = backward_hidden(
        grad, two_full_one, kept_one, hidden_weights
    )
    hidden_far, hidden_near = weight_grads(
        ids,
        (0, ((kept_one[3], inner_grad_one),)),
        (1, ((kept_one[5], two_full_one),)),
        base=hidden_base,
        far_first=True,
    )
    hidden_far = across(hidden_far, 3)
    one_full_one = whole(exchange(grad_copies))
    query_grad, own, sent = backward_attention(one_full_one, query_one, bundle_one)
    hidden_near, hidden_other = call(
        core_sums_kernel, (blocks, blocks), ids, hidden_near, hidden_far, behind=sent[:1]
    )
    (hidden_near,) = call(add_kernel, (blocks,), ids, hidden_near, core_swap(hidden_other))
    hidden_last = across(hidden_near, 1)
    qkv_grad_one, bias_grad_one, pieces = call(
        last_back_kernel,
        (((tokens, 3 * HEAD), BF), ((1, 3 * HEAD), F32), ((parts, tokens + 2 * own_rows + 16, features), BF)),
        ids,
        query_grad,
        own,
        *sent,
        qkv_weights,
        grad,
        last_rows,
        sums_a,
        sums_b,
        sums_c,
        sums_d,
        behind=(hidden_near,),
    )
    arrived = exchange(pieces)

    sent, kept = weight_grads(
        ids,
        (0, ((acts_two, qkv_grad_two), (acts_one, qkv_grad_one))),
        (0, ((one_full, kept_two[0]), (one_full_one, kept_one[0]))),
    )
    near, far = call(core_sums_kernel, (block, block), ids, kept, core_swap(sent))
    near_sum, far_sum = near, far
    (near,) = call(add_kernel, (block,), ids, near, across(far, 3))

    two = ((2, tokens, features), F32)
    own, vector_sums = call(meet_kernel, (two, ((8, features), F32)), ids, arrived, behind=(far_sum,))
    bias_grads = (bias_grad_two + bias_grad_one)[0]
    small = jnp.concatenate([(hidden_bias_two + hidden_bias_one)[0], bias_grads, vector_sums.reshape(-1)])
    small = jnp.pad(small, (0, -small.shape[0] % (8 * features))).reshape(-1, features)
    rows_out = ((2 * tokens + small.shape[0], features), F32)
    kept, sent = call(keep_kernel, (rows_out, rows_out), ids, own, core_swap(own), small, core_swap(small))
    passed = across(sent, 1)
    small = kept[2 * tokens :] + passed[2 * tokens :]
    small = (small + across(small, 3)).reshape(-1)
    bias_at = hidden_size + 3 * HEAD
    vector_sums = small[bias_at : bias_at + 8 * features].reshape(8, features)
    boundary = jnp.where(core == section, kept[: 2 * tokens], passed[: 2 * tokens]).reshape(1, 2, tokens, features)

    attention_last = across(near, 1)
    in_sum, down_sum = hidden_sums(hidden_near, hidden_last, sent)
    square, wide = ((hidden_size, HEAD), F32), ((HEAD, hidden_size), F32)
    query_sum, key_sum, value_sum, out_sum = call(
        last_sums_kernel, (square, square, square, wide), ids, near, attention_last, behind=(in_sum, down_sum)
    )

    return (
        boundary,
        query_sum,
        key_sum,
        value_sum,
        small[hidden_size : hidden_size + HEAD],
        small[hidden_size + 2 * HEAD : bias_at],
        out_sum,
        vector_sums[0],
        vector_sums[1],
        vector_sums[2],
        in_sum,
        small[:hidden_size],
        down_sum,
        vector_sums[3],
        vector_sums[4],
        vector_sums[5],
    )


def solution(mesh):
    return jax.shard_map(
        body,
        mesh=mesh,
        in_specs=(
            P(None, "dp", "mp"),
            P(None, "dp", "mp"),
            P(),
            P("dp", "mp"),
            P("dp", "mp"),
            P("dp", "mp"),
            P("mp"),
            P("mp"),
            P("mp", "dp"),
            P("mp"),
            P("mp"),
            P("mp"),
            P("dp", "mp"),
            P("mp"),
            P("mp", "dp"),
            P("mp"),
            P("mp"),
            P("mp"),
        ),
        out_specs=(
            P("section", None, "dp", "mp"),
            P("dp", "mp"),
            P("dp", "mp"),
            P("dp", "mp"),
            P("mp"),
            P("mp"),
            P("mp", "dp"),
            P("mp"),
            P("mp"),
            P("mp"),
            P("dp", "mp"),
            P("mp"),
            P("mp", "dp"),
            P("mp"),
            P("mp"),
            P("mp"),
        ),
        check_vma=False,
    )
```

```python
import functools
import math

import jax
import jax.numpy as jnp
from jax import lax
from jax.experimental import pallas as pl
from jax.experimental.pallas import tpu as pltpu
from jax.sharding import PartitionSpec as P

HEAD = 128
SCALE = 1.0 / math.sqrt(HEAD)
EPS = 1e-06
BF = jnp.bfloat16
F32 = jnp.float32
STEPS = (0, 1, 3, 2)


def core_swap(array):
    count = lax.axis_size("dp")
    return lax.ppermute(array, "dp", [(i, i ^ 1) for i in range(count)])


def across(array, bits):
    count = lax.axis_size("dp")
    route = []
    for s in range(2):
        for i in range(count):
            x = (2 * (i // 2) + s) ^ bits
            route.append((s * count + i, (x % 2) * count + 2 * (x // 2) + i % 2))
    return lax.ppermute(array, ("section", "dp"), route)


def exchange(pieces):
    return lax.all_to_all(pieces, "mp", split_axis=0, concat_axis=0, tiled=True)


def after(array, *others):
    return lax.optimization_barrier((array, *others))[0]


def four_blocks(own, far):
    return own, core_swap(own), far, core_swap(far)


def split_terms(value):
    high = value.astype(BF)
    return high, (value - high.astype(F32)).astype(BF)


def dot(left, right):
    return jnp.dot(left, right, preferred_element_type=F32)


def dot_t(left, right):
    return lax.dot_general(left, right, (((1,), (1,)), ((), ())), preferred_element_type=F32)


def t_dot(left, right):
    return lax.dot_general(left, right, (((0,), (0,)), ((), ())), preferred_element_type=F32)


def gelu_tanh(value):
    inner = math.sqrt(2.0 / math.pi) * (value + 0.044715 * (value * value * value))
    bend = jnp.tanh(inner)
    slope = math.sqrt(2.0 / math.pi) * (1.0 + 3.0 * 0.044715 * (value * value))
    return 0.5 * value * (1.0 + bend), 0.5 * (1.0 + bend) + 0.5 * value * (1.0 - bend * bend) * slope


def call(kernel, outs, ids, *arrays, behind=()):
    count = len(arrays)

    def body(ids, *refs):
        kernel(ids, *refs[:count], *refs[count + len(behind) :])

    in_specs = [pl.BlockSpec(memory_space=pltpu.SMEM)] + [pl.BlockSpec(memory_space=pltpu.VMEM)] * count
    return pl.pallas_call(
        body,
        in_specs=in_specs + [pl.BlockSpec(memory_space=pl.ANY)] * len(behind),
        out_specs=[pl.BlockSpec(memory_space=pltpu.VMEM)] * len(outs),
        out_shape=[jax.ShapeDtypeStruct(shape, dtype) for shape, dtype in outs],
        compiler_params=pltpu.CompilerParams(vmem_limit_bytes=40 * 2**20),
    )(ids, *arrays, *behind)


def gate(array, *behind):
    return pl.pallas_call(
        lambda *refs: None,
        in_specs=[pl.BlockSpec(memory_space=pl.ANY)] * (1 + len(behind)),
        out_specs=pl.BlockSpec(memory_space=pl.ANY),
        out_shape=jax.ShapeDtypeStruct(array.shape, array.dtype),
        input_output_aliases={0: 0},
    )(array, *behind)


def columns_of(ids, k, width):
    return pl.ds(pl.multiple_of((ids[0] ^ k) * width, width), width)


def mask_of(ids, tokens, bits):
    def labels(place, shape, dim):
        places = place * tokens + lax.broadcasted_iota(jnp.int32, shape, dim)
        return sum((places >= ids[3 + j]).astype(jnp.int32) for j in range(4))

    return labels(ids[1], (tokens, 1), 0) == labels(ids[1] ^ bits, (1, tokens), 1)


def probabilities(ids, query, key_refs):
    scores = []
    for bits, ref in zip(STEPS, key_refs):
        same = mask_of(ids, query.shape[0], bits)
        scores.append(jnp.where(same, dot_t(query, ref[:, :HEAD]) * SCALE, -1e30))
    top = functools.reduce(jnp.maximum, [jnp.max(score, axis=-1, keepdims=True) for score in scores])
    expo = [jnp.exp(score - top) for score in scores]
    total = sum(jnp.sum(e, axis=-1, keepdims=True) for e in expo)
    return [e / total for e in expo]


def pack_kernel(own_rows, ids, own_input, other_input, own_cotangent, other_cotangent, vectors, pieces):
    core, same = ids[7], ids[7] == ids[8]
    parts, _, features = pieces.shape
    tokens = own_input.shape[1]
    values = jnp.where(same, own_input[core].astype(F32), other_input[core].astype(F32)).astype(BF)
    cotangent = jnp.where(same, own_cotangent[core], other_cotangent[core])
    vector_terms = jnp.concatenate(split_terms(vectors[...]), axis=0)
    for r in range(parts):
        pieces[r, :tokens, :] = values
        at = tokens
        for term in (*split_terms(cotangent[r * own_rows : (r + 1) * own_rows]), vector_terms):
            pieces[r, at : at + term.shape[0], :] = term
            at += term.shape[0]


def unpack_kernel(own_rows, ids, arrived, acts, rows, cotangent, vectors):
    parts, _, features = arrived.shape
    tokens = acts.shape[0]
    count = vectors.shape[0]
    for r in range(parts):
        columns = slice(r * features, (r + 1) * features)
        acts[:, columns] = arrived[r, :tokens, :]
        high, low, both = (
            arrived[r, tokens + k * own_rows : tokens + (k + 1) * own_rows, :].astype(F32) for k in range(3)
        )
        cotangent[:, columns] = high + low
        vectors[:, columns] = both[:count] + both[count:]
    rows[...] = acts[pl.ds(pl.multiple_of(ids[2] * own_rows, own_rows), own_rows), :].astype(F32)


def bundle_kernel(ids, *refs):
    bundle = refs[-1]
    for k in range(4):
        for j in range(3):
            bundle[k, :, j * HEAD : (j + 1) * HEAD] = refs[3 * k + j][...]


def project_kernel(ids, acts, query_bias, pair_bias, weights, query, pair):
    total = 0.0
    for k in range(4):
        total = total + dot(acts[:, columns_of(ids, k, weights.shape[1])], weights[k])
    query[...] = (total[:, :HEAD] + query_bias[...]).astype(BF)
    pair[...] = (total[:, HEAD:] + pair_bias[...]).astype(BF)


def attend_kernel(ids, query, *refs):
    pairs, weights, (mixed, partial, bundle) = refs[:4], refs[4], refs[5:]
    for k, ref in enumerate(pairs):
        bundle[k] = ref[...]
    probs = probabilities(ids, query[...], pairs)
    value = sum(dot(p.astype(BF), ref[:, HEAD:]) for p, ref in zip(probs, pairs)).astype(BF)
    mixed[...] = value
    for k in range(4):
        partial[:, columns_of(ids, k, weights.shape[2])] = dot(value, weights[k]).astype(BF)


def hidden_kernel(ids, normed, bias, *refs):
    rising, falling, (inner, active, partial) = refs[:4], refs[4:8], refs[8:]
    total = bias[...]
    for k, ref in enumerate(rising):
        total = total + dot(normed[:, columns_of(ids, k, ref.shape[0])], ref[...])
    inner[...] = total
    value = gelu_tanh(total)[0].astype(BF)
    active[...] = value
    for k, ref in enumerate(falling):
        partial[:, columns_of(ids, k, ref.shape[1])] = dot(value, ref[...]).astype(BF)


def hidden_back_kernel(ids, grad, inner, *refs):
    rising, falling, (inner_grad, bias_grad, partial) = refs[:4], refs[4:8], refs[8:]
    total = 0.0
    for k, ref in enumerate(falling):
        total = total + dot_t(grad[:, columns_of(ids, k, ref.shape[1])], ref[...])
    value = (total * gelu_tanh(inner[...])[1]).astype(BF)
    inner_grad[...] = value
    bias_grad[...] = jnp.sum(value.astype(F32), axis=0, keepdims=True)
    for k, ref in enumerate(rising):
        partial[:, columns_of(ids, k, ref.shape[0])] = dot_t(value, ref[...]).astype(BF)


def attend_back_kernel(ids, grad, query, bundle, weights, query_grad, own, *sent):
    pairs = [bundle.at[k] for k in range(4)]
    mixed_grad = 0.0
    for k in range(4):
        mixed_grad = mixed_grad + dot_t(grad[:, columns_of(ids, k, weights.shape[2])], weights[k])
    mixed_grad = mixed_grad.astype(BF)
    probs = probabilities(ids, query[...], pairs)
    prob_grads = [dot_t(mixed_grad, ref[:, HEAD:]) for ref in pairs]
    inside = sum(jnp.sum(p * g, axis=-1, keepdims=True) for p, g in zip(probs, prob_grads))
    score_grads = [(p * (g - inside)).astype(BF) for p, g in zip(probs, prob_grads)]
    query_grad[...] = (sum(dot(s, ref[:, :HEAD]) for s, ref in zip(score_grads, pairs)) * SCALE).astype(BF)
    for s, p, ref in zip(score_grads, probs, (own, *sent)):
        ref[:, :HEAD] = (t_dot(s, query[...]) * SCALE).astype(ref.dtype)
        ref[:, HEAD:] = t_dot(p.astype(BF), mixed_grad).astype(ref.dtype)


def joined_grads(query_grad, own, arrived, qkv_grad, bias_grad):
    pair = own[...]
    for ref in arrived:
        pair = pair + ref[...].astype(F32)
    value = jnp.concatenate([query_grad[...], pair.astype(BF)], axis=1)
    qkv_grad[...] = value
    bias_grad[...] = jnp.sum(value.astype(F32), axis=0, keepdims=True)
    return value


def project_back_kernel(ids, query_grad, own, *refs):
    arrived, weights, (qkv_grad, bias_grad, partial) = refs[:3], refs[3], refs[4:]
    value = joined_grads(query_grad, own, arrived, qkv_grad, bias_grad)
    for k in range(4):
        partial[:, columns_of(ids, k, weights.shape[1])] = dot_t(value, weights[k]).astype(BF)


def last_back_kernel(ids, query_grad, own, *refs):
    arrived, weights, (grad, last_rows), vector_refs = refs[:3], refs[3], refs[4:6], refs[6:10]
    qkv_grad, bias_grad, pieces = refs[10:]
    value = joined_grads(query_grad, own, arrived, qkv_grad, bias_grad)
    tokens, own_rows = value.shape[0], grad.shape[0]
    row = lax.broadcasted_iota(jnp.int32, (tokens, 1), 0) // own_rows
    for k in range(4):
        weight = weights[k]
        block = dot_t(value, weight)
        own_block = grad[:, columns_of(ids, k, weight.shape[0])]
        repeated = jnp.concatenate([own_block] * (tokens // own_rows), axis=0)
        block = jnp.where(row == ids[2], block + repeated, block).astype(BF)
        for j in range(weight.shape[0] // HEAD):
            pieces[(ids[0] ^ k) * (weight.shape[0] // HEAD) + j, :tokens, :] = block[:, j * HEAD : (j + 1) * HEAD]
    for r in range(pieces.shape[0]):
        columns = slice(r * HEAD, (r + 1) * HEAD)
        high, low = split_terms(last_rows[:, columns])
        pieces[r, tokens : tokens + own_rows, :] = high
        pieces[r, tokens + own_rows : tokens + 2 * own_rows, :] = low
        terms = split_terms(sum(ref[:, columns] for ref in vector_refs))
        pieces[r, tokens + 2 * own_rows : tokens + 2 * own_rows + 16, :] = jnp.concatenate(terms, axis=0)


def norm_of(value, gain, shift):
    mean = jnp.mean(value, axis=-1, keepdims=True)
    centered = value - mean
    rstd = lax.rsqrt(jnp.mean(centered * centered, axis=-1, keepdims=True) + EPS)
    standard = centered * rstd
    return standard * gain + shift, standard, rstd


def norm_back(grad, standard, rstd, gain):
    scaled = grad * gain
    mean = jnp.mean(scaled, axis=-1, keepdims=True)
    cross = jnp.mean(scaled * standard, axis=-1, keepdims=True)
    return rstd * (scaled - mean - standard * cross)


def to_all(copies, value):
    low = value.astype(BF)
    for r in range(copies.shape[0]):
        copies[r] = low


def summed(arrived):
    total = arrived[0].astype(F32)
    for r in range(1, arrived.shape[0]):
        total = total + arrived[r].astype(F32)
    return total


def column_sums(first, grad, standard, back):
    row = lax.broadcasted_iota(jnp.int32, (8, grad.shape[1]), 0)
    total = jnp.zeros((8, grad.shape[1]), F32)
    for k, value in enumerate((back, grad * standard, grad)):
        total = jnp.where(row == first + k, jnp.sum(value, axis=0, keepdims=True), total)
    return total


def norm_kernel(first, ids, arrived, residual, vectors, result, standard, rstd, copies):
    bias, gain, shift = (vectors[first + k : first + k + 1, :] for k in range(3))
    value, standard_rows, rstd_rows = norm_of(residual[...] + summed(arrived) + bias, gain, shift)
    to_all(copies, value)
    result[...], standard[...] = value, standard_rows
    rstd[...] = jnp.broadcast_to(rstd_rows, rstd.shape)


def norm_back_kernel(first, ids, arrived, residual, standard, rstd, vectors, back, sums, copies):
    grad = residual[...] + summed(arrived)
    value = norm_back(grad, standard[...], rstd[:, :1], vectors[first + 1 : first + 2, :])
    to_all(copies, value)
    back[...] = value
    sums[...] = column_sums(first, grad, standard[...], value)


def norm_back_and_sums_kernel(first, ids, arrived, residual, standard, rstd, vectors, kept, swapped, *outs):
    norm_back_kernel(first, ids, arrived, residual, standard, rstd, vectors, *outs[:3])
    core_sums_kernel(ids, kept, swapped, *outs[3:])


def turn_kernel(ids, arrived, residual, cotangent, vectors, result, back, sums, copies):
    bias, gain, shift = (vectors[3 + k : 4 + k, :] for k in range(3))
    value, standard, rstd = norm_of(residual[...] + summed(arrived) + bias, gain, shift)
    result[...] = value
    grad = cotangent[...]
    value = norm_back(grad, standard, rstd, gain)
    to_all(copies, value)
    back[...] = value
    sums[...] = column_sums(3, grad, standard, value)


def meet_kernel(ids, arrived, both, vectors):
    parts, _, features = arrived.shape
    tokens = both.shape[1]
    own_rows = tokens // parts
    total, last = 0.0, 0.0
    for r in range(parts):
        total = total + arrived[r, :tokens, :].astype(F32)
        high, low, terms = (
            arrived[r, tokens + k * own_rows : tokens + (k + 1) * own_rows, :].astype(F32) for k in range(3)
        )
        both[1, r * own_rows : (r + 1) * own_rows, :] = high + low
        last = last + terms
    both[0] = total
    vectors[...] = last[:8] + last[8:]


def keep_kernel(ids, own, other, own_small, other_small, kept, sent):
    core, section = ids[7], ids[8]
    tokens = own.shape[1]
    rows = own_small.shape[0]
    total = own_small[...] + other_small[...]
    kept[2 * tokens :, :] = total
    sent[2 * tokens :, :] = total
    for ref, index in ((kept, section), (sent, 1 - section)):
        ref[pl.ds(pl.multiple_of(core * tokens, tokens), tokens), :] = own[index]
        ref[pl.ds(pl.multiple_of((1 - core) * tokens, tokens), tokens), :] = other[index]


def weight_grads(ids, *products, base=(), behind=(), far_first=False):
    tokens = products[0][1][0][0].shape[0]
    shapes = []
    for axis, pairs in products:
        shape = [pairs[0][0].shape[1], pairs[0][1].shape[1]]
        shape[axis] //= 4
        shapes.append(tuple(shape))
    stacked = len(shapes) > 1 and len(set(shapes)) == 1
    if base:
        whole_shape = base[0].shape[1:]
    elif stacked:
        whole_shape = (len(shapes), *shapes[0])
    else:
        whole_shape = (shapes[0][0], sum(shape[1] for shape in shapes))

    def kernel(ids, *refs):
        parts, at = [], 0
        for _, pairs in products:
            parts.append(sum(t_dot(refs[at + 2 * j][...], refs[at + 2 * j + 1][...]) for j in range(len(pairs))))
            at += 2 * len(pairs)

        def store(ref, earlier):
            if stacked:
                for j, part in enumerate(parts):
                    ref[0, j] = (part if earlier is None else part + earlier[0, j].astype(F32)).astype(BF)
            else:
                part = jnp.concatenate(parts, axis=1)
                width = part.shape[1]
                if earlier is not None:
                    part = part + earlier[0, :, :width].astype(F32)
                    if width < whole_shape[1]:
                        ref[0, :, width:] = earlier[0, :, width:]
                ref[0, :, :width] = part.astype(BF)

        earlier = refs[at : at + 2] if base else (None, None)
        pl.when(pl.program_id(0) < 2)(lambda: store(refs[-2], earlier[0]))
        pl.when(pl.program_id(0) >= 2)(lambda: store(refs[-1], earlier[1]))

    def cut(i, ids):
        order = jnp.where(i < 2, i + 2, i - 2) if far_first else jnp.where(i < 2, 2 * i + 1, 2 * i - 4)
        return (0, ids[0] ^ order)

    def whole(i, ids):
        return (0, 0)

    zeros = (0,) * len(whole_shape)
    specs = [
        pl.BlockSpec((tokens, shape[side]), cut if side == axis else whole)
        for (axis, pairs), shape in zip(products, shapes)
        for _ in pairs
        for side in range(2)
    ]
    shares = [
        pl.BlockSpec((1, *whole_shape), lambda i, ids: (jnp.minimum(i, 1), *zeros)),
        pl.BlockSpec((1, *whole_shape), lambda i, ids: (jnp.maximum(i - 2, 0), *zeros)),
    ]
    return pl.pallas_call(
        kernel,
        grid_spec=pltpu.PrefetchScalarGridSpec(
            num_scalar_prefetch=1,
            grid=(4,),
            in_specs=specs + (shares if base else []) + [pl.BlockSpec(memory_space=pl.ANY)] * len(behind),
            out_specs=shares,
        ),
        out_shape=[jax.ShapeDtypeStruct((2, *whole_shape), BF)] * 2,
        compiler_params=pltpu.CompilerParams(vmem_limit_bytes=40 * 2**20),
    )(ids, *[array for _, pairs in products for pair in pairs for array in pair], *base, *behind)


def add_kernel(ids, left, right, total):
    total[...] = (left[...].astype(F32) + right[...].astype(F32)).astype(total.dtype)


def hidden_sums(left, right, behind):
    _, rows, columns = left.shape

    def kernel(left, right, _, first, second, held, leaving):
        copies = []
        for j, ref in enumerate((first, second)):
            held[j] = left[j].astype(F32) + right[j].astype(F32)
            copies.append(pltpu.make_async_copy(held.at[j], ref, leaving.at[j]))
            copies[j].start()
        for copy in copies:
            copy.wait()

    return pl.pallas_call(
        kernel,
        in_specs=[pl.BlockSpec(memory_space=pltpu.VMEM)] * 2 + [pl.BlockSpec(memory_space=pl.ANY)],
        out_specs=[pl.BlockSpec(memory_space=pltpu.HBM)] * 2,
        out_shape=[jax.ShapeDtypeStruct((rows, columns), F32)] * 2,
        scratch_shapes=[pltpu.VMEM(left.shape, F32), pltpu.SemaphoreType.DMA((2,))],
        compiler_params=pltpu.CompilerParams(vmem_limit_bytes=40 * 2**20),
    )(left, right, behind)


def core_sums_kernel(ids, kept, arrived, near, far):
    for j, ref in enumerate((near, far)):
        ref[...] = (kept[j].astype(F32) + arrived[j].astype(F32)).astype(BF)


def last_sums_kernel(ids, left, right, query, key, value, out):
    for j, ref in enumerate((query, key, value)):
        columns = slice(j * HEAD, (j + 1) * HEAD)
        ref[...] = left[:, columns].astype(F32) + right[:, columns].astype(F32)
    out[...] = (left[:, 3 * HEAD :].astype(F32) + right[:, 3 * HEAD :].astype(F32)).T


def body(
    layer_input,
    out_cotangent,
    doc_lengths,
    query_weight,
    key_weight,
    value_weight,
    query_bias,
    value_bias,
    output_weight,
    output_bias,
    attention_norm_gain,
    attention_norm_shift,
    hidden_weight,
    hidden_bias,
    proj_weight,
    proj_bias,
    closing_norm_gain,
    closing_norm_shift,
):
    section = lax.axis_index("section")
    part = lax.axis_index("dp")
    place = lax.axis_index("mp")
    parts = lax.axis_size("mp")
    core = part % 2
    x = 2 * (part // 2) + section
    tokens, features = layer_input.shape[1:]
    own_rows = tokens // parts

    other_input, other_cotangent = core_swap(layer_input), core_swap(out_cotangent)

    qkv_far = [across(array, 3) for array in (query_weight, key_weight, value_weight)]
    out_far = across(output_weight, 3)
    qkv_blocks = [four_blocks(own, far) for own, far in zip((query_weight, key_weight, value_weight), qkv_far)]
    qkv_weights = [array for block in zip(*qkv_blocks) for array in block]
    out_weights = jnp.stack(four_blocks(output_weight, out_far))
    hidden_core = core_swap(hidden_weight), core_swap(proj_weight)

    vectors = jnp.stack(
        [output_bias, attention_norm_gain, attention_norm_shift, proj_bias, closing_norm_gain, closing_norm_shift]
    )
    bounds = jnp.cumsum(lax.dynamic_index_in_dim(doc_lengths, core, 0, keepdims=False)).astype(jnp.int32)
    ids = jnp.concatenate([jnp.stack([part, x, place]).astype(jnp.int32), bounds, jnp.stack([core, section]).astype(jnp.int32)])

    (arrived,) = call(
        functools.partial(pack_kernel, own_rows),
        (((parts, tokens + 2 * own_rows + 16, features), BF),),
        ids,
        layer_input,
        other_input,
        out_cotangent,
        other_cotangent,
        jnp.pad(vectors, ((0, 2), (0, 0))),
    )
    arrived = after(exchange(arrived), *hidden_core)

    width = parts * features
    full, some = ((tokens, width), BF), ((own_rows, width), F32)
    copies = ((parts, own_rows, width), BF)
    eight = ((8, width), F32)
    narrow = ((own_rows, HEAD), F32)
    pair_shape = (tokens, 2 * HEAD)
    hidden_size = hidden_bias.shape[0]

    block = ((hidden_size, hidden_size), BF)
    full_block = ((hidden_size, hidden_size), F32)
    blocks = ((2, hidden_size, hidden_size), BF)

    def cut_rows(partial):
        return partial.reshape(parts, own_rows, width)

    def whole(stack):
        return stack.reshape(tokens, width)

    hidden_own = (hidden_weight, proj_weight)
    hidden_stack = jnp.stack(hidden_own)
    (qkv_weights,) = call(bundle_kernel, (((4, 4 * HEAD, 3 * HEAD), BF),), ids, *qkv_weights)
    acts_one, rows, cotangent, vectors = call(
        functools.partial(unpack_kernel, own_rows), (full, some, some, eight), ids, arrived, behind=(hidden_stack,)
    )
    query_bias_row = query_bias[None]
    pair_bias_row = jnp.concatenate([jnp.zeros_like(value_bias), value_bias])[None]
    hidden_bias_row = hidden_bias[None]

    def keys_of(acts):
        query, pair = call(
            project_kernel,
            (((tokens, HEAD), BF), (pair_shape, BF)),
            ids,
            acts,
            query_bias_row,
            pair_bias_row,
            qkv_weights,
        )
        return query, [pair] + [across(pair, bits) for bits in STEPS[1:]]

    def forward(query, pairs, residual, weights_then):
        mixed, partial, bundle = call(
            attend_kernel,
            (((tokens, HEAD), BF), full, ((4, *pair_shape), BF)),
            ids,
            query,
            *pairs,
            out_weights,
        )
        arrived = exchange(cut_rows(partial))
        normed, standard, rstd, normed_copies = call(
            functools.partial(norm_kernel, 0), (some, some, narrow, copies), ids, arrived, residual, vectors
        )
        normed_copies, weights = weights_then(normed_copies, arrived)
        normed_full = whole(exchange(normed_copies))
        inner, active, partial = call(
            hidden_kernel,
            (((tokens, hidden_size), F32), ((tokens, hidden_size), BF), full),
            ids,
            normed_full,
            hidden_bias_row,
            *weights,
        )
        return exchange(cut_rows(partial)), normed, (mixed, standard, rstd, normed_full, inner, active), bundle

    def backward_hidden(grad, grad_full, kept, weights, beside=lambda inner_grad: ()):
        _, standard, rstd, _, inner, _ = kept
        inner_grad, bias_grad, partial = call(
            hidden_back_kernel,
            (((tokens, hidden_size), BF), ((1, hidden_size), F32), full),
            ids,
            grad_full,
            inner,
            *weights,
        )
        arrived = exchange(cut_rows(partial))
        shares = beside(inner_grad)
        back, sums, back_copies, *core_sums = call(
            functools.partial(norm_back_and_sums_kernel if shares else norm_back_kernel, 0),
            (some, eight, copies, *[blocks] * len(shares)),
            ids,
            arrived,
            grad,
            standard,
            rstd,
            vectors,
            *shares,
        )
        return back, sums, back_copies, inner_grad, bias_grad, *core_sums

    def backward_attention(grad_full, query, bundle, behind=()):
        query_grad, own, *sent = call(
            attend_back_kernel,
            (((tokens, HEAD), BF), (pair_shape, F32), *[(pair_shape, BF)] * 3),
            ids,
            grad_full,
            query,
            bundle,
            out_weights,
            behind=behind,
        )
        return query_grad, own, [across(array, bits) for array, bits in zip(sent, STEPS[1:])]

    query_one, pairs_one = keys_of(acts_one)
    hidden_far = across(hidden_stack, 3)
    hidden_weights = []

    def set_out(normed_copies, arrived):
        far = after(hidden_far, arrived)
        far = (far[0], far[1])
        far_core = [core_swap(array) for array in far]
        for j in range(2):
            hidden_weights.extend((hidden_own[j], hidden_core[j], far[j], far_core[j]))
        return after(normed_copies, *far_core), hidden_weights

    arrived, normed_one, kept_one, bundle_one = forward(query_one, pairs_one, rows, set_out)
    middle_rows, standard_one, rstd_one, row_copies = call(
        functools.partial(norm_kernel, 3), (some, some, narrow, copies), ids, arrived, normed_one, vectors
    )
    acts_two = whole(exchange(row_copies))
    query_two, pairs_two = keys_of(acts_two)
    arrived, normed_two, kept_two, bundle_two = forward(
        query_two, pairs_two, middle_rows, lambda normed_copies, arrived: (normed_copies, hidden_weights)
    )
    last_rows, grad, sums_a, grad_copies = call(
        turn_kernel, (some, some, eight, copies), ids, arrived, normed_two, cotangent, vectors
    )

    two_full = whole(exchange(grad_copies))
    grad, sums_b, grad_copies, inner_grad_two, hidden_bias_two = backward_hidden(grad, two_full, kept_two, hidden_weights)
    one_full = whole(exchange(grad_copies))
    query_grad, own, sent = backward_attention(one_full, query_two, bundle_two)
    hidden_base = weight_grads(
        ids,
        (0, ((kept_two[3], inner_grad_two),)),
        (1, ((kept_two[5], two_full),)),
        behind=sent[:1],
        far_first=True,
    )
    qkv_grad_two, bias_grad_two, partial = call(
        project_back_kernel,
        (((tokens, 3 * HEAD), BF), ((1, 3 * HEAD), F32), full),
        ids,
        query_grad,
        own,
        *sent,
        qkv_weights,
        behind=hidden_base[:1],
    )
    arrived = exchange(cut_rows(partial))
    grad, sums_c, grad_copies = call(
        functools.partial(norm_back_kernel, 3), (some, eight, copies), ids, arrived, grad, standard_one, rstd_one, vectors
    )

    two_full_one = whole(exchange(grad_copies))
    grad, sums_d, grad_copies, inner_grad_one, hidden_bias_one = backward_hidden(
        grad, two_full_one, kept_one, hidden_weights
    )
    hidden_far, hidden_near = weight_grads(
        ids,
        (0, ((kept_one[3], inner_grad_one),)),
        (1, ((kept_one[5], two_full_one),)),
        base=hidden_base,
        far_first=True,
    )
    hidden_far = across(hidden_far, 3)
    one_full_one = whole(exchange(grad_copies))
    query_grad, own, sent = backward_attention(one_full_one, query_one, bundle_one)
    hidden_near, hidden_other = call(
        core_sums_kernel, (blocks, blocks), ids, hidden_near, hidden_far, behind=sent[:1]
    )
    (hidden_near,) = call(add_kernel, (blocks,), ids, hidden_near, core_swap(hidden_other))
    hidden_last = across(hidden_near, 1)
    attention_base = weight_grads(
        ids,
        (0, ((acts_two, qkv_grad_two),)),
        (0, ((one_full, kept_two[0]), (one_full_one, kept_one[0]))),
        behind=sent[:1],
    )

    qkv_grad_one, bias_grad_one, pieces = call(
        last_back_kernel,
        (((tokens, 3 * HEAD), BF), ((1, 3 * HEAD), F32), ((parts, tokens + 2 * own_rows + 16, features), BF)),
        ids,
        query_grad,
        own,
        *sent,
        qkv_weights,
        grad,
        last_rows,
        sums_a,
        sums_b,
        sums_c,
        sums_d,
        behind=(attention_base[0], hidden_near),
    )
    arrived = exchange(pieces)

    sent, kept = weight_grads(ids, (0, ((acts_one, qkv_grad_one),)), base=attention_base)
    near, far = call(core_sums_kernel, (block, block), ids, kept, core_swap(sent))
    near_sum, far_sum = near, far
    (near,) = call(add_kernel, (block,), ids, near, across(far, 3))

    two = ((2, tokens, features), F32)
    own, vector_sums = call(meet_kernel, (two, ((8, features), F32)), ids, arrived, behind=(far_sum,))
    bias_grads = (bias_grad_two + bias_grad_one)[0]
    small = jnp.concatenate([(hidden_bias_two + hidden_bias_one)[0], bias_grads, vector_sums.reshape(-1)])
    small = jnp.pad(small, (0, -small.shape[0] % (8 * features))).reshape(-1, features)
    rows_out = ((2 * tokens + small.shape[0], features), F32)
    kept, sent = call(keep_kernel, (rows_out, rows_out), ids, own, core_swap(own), small, core_swap(small))
    passed = across(sent, 1)
    small = kept[2 * tokens :] + passed[2 * tokens :]
    small = (small + across(small, 3)).reshape(-1)
    bias_at = hidden_size + 3 * HEAD
    vector_sums = small[bias_at : bias_at + 8 * features].reshape(8, features)
    boundary = jnp.where(core == section, kept[: 2 * tokens], passed[: 2 * tokens]).reshape(1, 2, tokens, features)

    attention_last = across(near, 1)
    in_sum, down_sum = hidden_sums(hidden_near, hidden_last, sent)
    square, wide = ((hidden_size, HEAD), F32), ((HEAD, hidden_size), F32)
    query_sum, key_sum, value_sum, out_sum = call(
        last_sums_kernel, (square, square, square, wide), ids, near, attention_last, behind=(in_sum, down_sum)
    )

    return (
        boundary,
        query_sum,
        key_sum,
        value_sum,
        small[hidden_size : hidden_size + HEAD],
        small[hidden_size + 2 * HEAD : bias_at],
        out_sum,
        vector_sums[0],
        vector_sums[1],
        vector_sums[2],
        in_sum,
        small[:hidden_size],
        down_sum,
        vector_sums[3],
        vector_sums[4],
        vector_sums[5],
    )


def solution(mesh):
    return jax.shard_map(
        body,
        mesh=mesh,
        in_specs=(
            P(None, "dp", "mp"),
            P(None, "dp", "mp"),
            P(),
            P("dp", "mp"),
            P("dp", "mp"),
            P("dp", "mp"),
            P("mp"),
            P("mp"),
            P("mp", "dp"),
            P("mp"),
            P("mp"),
            P("mp"),
            P("dp", "mp"),
            P("mp"),
            P("mp", "dp"),
            P("mp"),
            P("mp"),
            P("mp"),
        ),
        out_specs=(
            P("section", None, "dp", "mp"),
            P("dp", "mp"),
            P("dp", "mp"),
            P("dp", "mp"),
            P("mp"),
            P("mp"),
            P("mp", "dp"),
            P("mp"),
            P("mp"),
            P("mp"),
            P("dp", "mp"),
            P("mp"),
            P("mp", "dp"),
            P("mp"),
            P("mp"),
            P("mp"),
        ),
        check_vma=False,
    )
```
